128 devices in a mesh: row: 32 (over x, y, core), col: 4 (over z).
Axes of the slice: x: 4, y: 4, z: 4, core: 2. Of those that a mesh axis runs over, the one named last changes fastest.
Arguments:
- block_values: bfloat16 [32, 4, 64, 256, 256], P('row', 'col'), may hold values from -0.1875 to 0.1875
- block_rows: int32 [32, 4, 64], P('row', 'col'), may hold values from 0 to 63
- block_cols: int32 [32, 4, 64], P('row', 'col'), may hold values from 0 to 255
- live_count: int32 [32, 4], P('row', 'col'), may hold values from 16 to 64, as said below
- objective: float32 [262144], P('col'), may hold values from -6 to 6
- upper_bound: float32 [262144], P('col'), may hold values from 0.5 to 2
- demand: float32 [524288], P('row'), may hold values from -6 to 6
- primal_start: float32 [262144], P('col'), may hold values from 0 to 0.5
- dual_start: float32 [524288], P('row'), may hold values from 0 to 0.5
- restart_at: int32 [8], replicated, may hold values 0 or 1
Outputs:
- primal_final: float32 [262144], P('col')
- dual_final: float32 [524288], P('row')
The draws below stay inside these ranges and needn't reach their ends.
Inputs may be any that keep to these rules, and one draw needn't show every extreme that they name: `live_count`: each device's count of used slots; some device uses all 64.
All inputs are finite; a program needn't handle non-finite values.
Results may differ from the reference program's by a relative error of at most 0.0018.
Values may be sent and summed in bfloat16 or wider, within the bound.
No kernel may reach another device: no remote copies, remote signals or barrier semaphores. Data moves between devices by JAX's collectives and lax.ppermute only.
A program may use at most 64 MiB of HBM per device.

```python
import math
import jax
import jax.numpy as jnp
from jax import lax

BS = 256
NB = 64
RB = 64
CB = 256
ITERS = 8
ROWS = 524288
COLS = 262144
N_ROW = 32
N_COL = 4


def draw_live_count(key, part):
    base_counts = jax.random.randint(key, (N_ROW * N_COL,), NB // 4, NB + 1)
    chosen = jax.random.randint(jax.random.fold_in(key, 7), (), 0, N_ROW * N_COL)
    filled = jnp.where(jnp.arange(N_ROW * N_COL) == chosen, NB, base_counts)
    return filled.reshape(N_ROW, N_COL).astype(jnp.int32)


def with_ends(result, rng, low, high):
    longest = result.shape.index(max(result.shape))
    spots = []
    for shift in (0, 1):
        where = [jax.random.randint(jax.random.fold_in(rng, axis), (), 0, length) for axis, length in enumerate(result.shape)]
        where[longest] = (where[longest] + shift) % result.shape[longest]
        spots.append(tuple(where))
    return result.at[spots[0]].set(low).at[spots[1]].set(high)


def levels(stream_key, extent, split, smallest, largest):
    def one(dim, shards_of):
        steps = jax.random.uniform(jax.random.fold_in(jax.random.fold_in(stream_key, 6), dim), (shards_of,), jnp.float32, smallest / len(split), largest / len(split))
        return jnp.repeat(jnp.exp(steps), extent[dim] // shards_of).reshape((-1,) + (1,) * (len(extent) - dim - 1))

    factor_of = one(*split[0])
    for cut in split[1:]:
        factor_of = factor_of * one(*cut)
    return factor_of


def noise(own_key, extent, scale, reach, cuts=(), kind=jnp.bfloat16):
    array = jax.random.normal(own_key, extent, jnp.float32) * scale
    if len(cuts) > 0:
        array = levels(own_key, extent, cuts, -0.22, 0.18) * array
    return jnp.clip(array, min=-reach, max=reach).astype(kind)


def setup_inputs(seed: int = 0) -> dict:
    splits = jax.random.split(jax.random.key(seed), 11)
    return {
        "block_values": noise(splits[0], (N_ROW, N_COL, NB, BS, BS), (4 * BS) ** -0.5, 0.1875, ((0, 32), (1, 4))),
        "block_rows": with_ends(jax.random.randint(splits[1], (N_ROW, N_COL, NB), 0, RB), jax.random.fold_in(splits[1], 1), 0, RB - 1).astype(jnp.int32),
        "block_cols": with_ends(jax.random.randint(splits[2], (N_ROW, N_COL, NB), 0, CB), jax.random.fold_in(splits[2], 1), 0, CB - 1).astype(jnp.int32),
        "live_count": draw_live_count(jax.random.fold_in(splits[10], 71), 0),
        "objective": noise(splits[4], (COLS,), 1.0, 6.0, ((0, 4),), jnp.float32),
        "upper_bound": jnp.clip(jnp.exp(math.log(2.0) - 1.3862944 * jax.random.uniform(splits[5], (COLS,), jnp.float32) ** levels(splits[5], (COLS,), ((0, 4),), -0.2, 0.2)), 0.5, 2.0),
        "demand": noise(splits[6], (ROWS,), 1.0, 6.0, ((0, 32),), jnp.float32),
        "primal_start": jnp.clip(0.5 * jax.random.uniform(splits[7], (COLS,), jnp.float32) ** levels(splits[7], (COLS,), ((0, 4),), -0.2, 0.2), 0.0, 0.5),
        "dual_start": jnp.clip(0.5 * jax.random.uniform(splits[8], (ROWS,), jnp.float32) ** levels(splits[8], (ROWS,), ((0, 32),), -0.2, 0.2), 0.0, 0.5),
        "restart_at": with_ends((jax.random.randint(splits[9], (ITERS,), 0, 2) < 1).astype(jnp.int32), jax.random.fold_in(splits[9], 1), 0, 1),
    }


step_scale = 0.3
epsilon = 1e-06

def dual_part(slot_values, rows_index, cols_index, used_slots, y_group):
    slots = slot_values.shape[0]
    block_size = slot_values.shape[1]
    live_slot = (jnp.arange(slots, dtype=jnp.int32) < used_slots).astype(jnp.float32)
    pieces = y_group.astype(jnp.bfloat16).reshape(-1, block_size)[rows_index].astype(jnp.float32)
    products = jnp.einsum('tij,ti->tj', slot_values.astype(jnp.float32), pieces, precision=lax.Precision.HIGHEST)
    products = products * live_slot[:, None]
    return jax.ops.segment_sum(products, cols_index, num_segments=CB).reshape(-1)

def primal_part(slot_values, rows_index, cols_index, used_slots, x_group):
    slots = slot_values.shape[0]
    block_size = slot_values.shape[1]
    live_slot = (jnp.arange(slots, dtype=jnp.int32) < used_slots).astype(jnp.float32)
    pieces = x_group.reshape(-1, block_size)[cols_index].astype(jnp.float32)
    products = jnp.einsum('tij,tj->ti', slot_values.astype(jnp.float32), pieces, precision=lax.Precision.HIGHEST)
    products = products * live_slot[:, None]
    return jax.ops.segment_sum(products, rows_index, num_segments=RB).reshape(-1)

def reference(block_values, block_rows, block_cols, live_count, objective, upper_bound, demand, primal_start, dual_start, restart_at):

    def dual_total(y):
        y_groups = y.reshape(N_ROW, -1)

        def step_fn(accum, r):
            part = jax.vmap(dual_part, in_axes=(0, 0, 0, 0, None))(block_values[r], block_rows[r], block_cols[r], live_count[r], y_groups[r])
            return (accum + part.reshape(-1), None)
        accum, unused = lax.scan(step_fn, jnp.zeros((COLS,), jnp.float32), jnp.arange(N_ROW, dtype=jnp.int32))
        return accum

    def primal_total(extrap_low):
        x_groups = extrap_low.reshape(N_COL, -1)

        def step_fn(carry, r):
            part = jax.vmap(primal_part, in_axes=(0, 0, 0, 0, 0))(block_values[r], block_rows[r], block_cols[r], live_count[r], x_groups)
            return (carry, lax.optimization_barrier(jnp.sum(part, axis=0)))
        carry, stacked = lax.scan(step_fn, jnp.zeros((), jnp.float32), jnp.arange(N_ROW, dtype=jnp.int32))
        return stacked.reshape(-1)
    x = primal_start
    y = dual_start
    anchor_x = x
    anchor_y = y
    sum_x = jnp.zeros_like(x)
    sum_y = jnp.zeros_like(y)
    taken = jnp.zeros((), jnp.float32)
    omega = jnp.ones((), jnp.float32)
    for k in range(ITERS):
        step_primal = step_scale / omega
        step_dual = step_scale * omega
        dual_image = dual_total(y)
        x_next = jnp.minimum(jnp.maximum(x - step_primal * (objective - dual_image), 0.0), upper_bound)
        extrap_low = (2.0 * x_next - x).astype(jnp.bfloat16)
        primal_image = primal_total(extrap_low)
        y_next = jnp.maximum(y + step_dual * (demand - primal_image), 0.0)
        x = x_next
        y = y_next
        sum_x = sum_x + x
        sum_y = sum_y + y
        taken = taken + 1.0
        if k <= ITERS - 3:
            is_restart = restart_at[k] == 1
            mean_x = sum_x / taken
            mean_y = sum_y / taken
            drift_x = jnp.sum((mean_x - anchor_x) ** 2) / COLS + epsilon
            drift_y = jnp.sum((mean_y - anchor_y) ** 2) / ROWS + epsilon
            omega_next = jnp.sqrt(omega) * (drift_x / drift_y) ** 0.25
            x = jnp.where(is_restart, mean_x, x)
            y = jnp.where(is_restart, mean_y, y)
            anchor_x = jnp.where(is_restart, mean_x, anchor_x)
            anchor_y = jnp.where(is_restart, mean_y, anchor_y)
            sum_x = jnp.where(is_restart, jnp.zeros_like(sum_x), sum_x)
            sum_y = jnp.where(is_restart, jnp.zeros_like(sum_y), sum_y)
            taken = jnp.where(is_restart, jnp.zeros_like(taken), taken)
            omega = jnp.where(is_restart, omega_next, omega)
    return (x, y)
```

```python
import functools

import jax
import jax.numpy as jnp
from jax import lax
from jax.experimental import pallas as pl
from jax.experimental.pallas import tpu as pltpu
from jax.sharding import Mesh
from jax.sharding import PartitionSpec as P

ITERS = 8
XY = ("row_0", "row_1")
CORE = "row_2"
ROW = ("row_0", "row_1", "row_2")
MESSAGE_ROWS = 80

step_scale = 0.3
epsilon = 1e-06

f32, bf16 = jnp.float32, jnp.bfloat16
SCALARS = pl.BlockSpec(memory_space=pltpu.SMEM)
VECTORS = pl.BlockSpec(memory_space=pltpu.VMEM)


def call(body, name, scalars, arrays, outs, scratch=(), flops=0):
    moved = sum(a.size * a.dtype.itemsize for a in arrays)
    return pl.pallas_call(
        body,
        name=name,
        in_specs=[SCALARS] * len(scalars) + [VECTORS] * len(arrays),
        out_specs=[VECTORS] * len(outs),
        out_shape=[jax.ShapeDtypeStruct(s, t) for s, t in outs],
        scratch_shapes=[pltpu.VMEM(s, t) for s, t in scratch],
        compiler_params=pltpu.CompilerParams(vmem_limit_bytes=24 << 20),
        cost_estimate=pl.CostEstimate(flops=flops, bytes_accessed=moved, transcendentals=0),
    )(*scalars, *arrays)


def products(index, source, blocks, target, contract):
    def step(t, carry):
        piece = source[pl.ds(index[t], 1), :].astype(bf16)
        target[pl.ds(t, 1), :] = lax.dot_general(
            piece, blocks[t], (((1,), (contract,)), ((), ())), preferred_element_type=f32
        )
        return carry

    lax.fori_loop(0, blocks.shape[0], step, 0, unroll=True)


def in_rows(total, first):
    row = lax.broadcasted_iota(jnp.int32, (16, 256), 0)
    whole = jnp.full((16, 256), total, f32)
    high = whole.astype(bf16).astype(f32)
    middle = (whole - high).astype(bf16).astype(f32)
    low = whole - high - middle
    zero = jnp.zeros_like(whole)
    return jnp.where(
        row == first,
        high,
        jnp.where(row == first + 1, middle, jnp.where(row == first + 2, low, zero)),
    )


def taken_by(restart, k):
    taken = jnp.int32(1)
    for j in range(k):
        taken = jnp.where(restart[j] == 1, 1, taken + 1)
    return taken.astype(f32)


def to_peers(live, found, extra, message):
    slot = lax.broadcasted_iota(jnp.int32, found.shape, 0)
    kept = jnp.where(slot < live[0], found[...], 0.0).astype(bf16)
    tail = extra.astype(bf16)
    for p in range(message.shape[0]):
        message[p, : found.shape[0], :] = kept
        message[p, found.shape[0] :, :] = tail


def first_dual(rows, live, cols_row, y, blocks, message, found):
    products(rows, y, blocks, found, 0)
    row = lax.broadcasted_iota(jnp.int32, (16, 256), 0)
    extra = jnp.where(row == 0, jnp.broadcast_to(cols_row[0:1, :], (16, 256)), 0.0)
    to_peers(live, found, extra, message)


def sum_columns(chosen, arrived, half):
    n = chosen.shape[0]
    half[0:n, :] = jnp.dot(chosen[...], arrived[...], preferred_element_type=f32)
    tail = jnp.zeros((16, 256), f32)
    for first in range(0, arrived.shape[0], MESSAGE_ROWS):
        tail = tail + arrived[first + MESSAGE_ROWS - 16 : first + MESSAGE_ROWS, :].astype(f32)
    total = tail[1:2, :] + tail[2:3, :] + tail[3:4, :]
    half[n : n + 8, :] = jnp.broadcast_to(total, (8, 256))


def primal_step(
    k,
    total_cols,
    total_rows,
    restart,
    cols,
    here,
    there,
    cost,
    bound,
    x_ref,
    sum_ref,
    anchor_ref,
    omega_ref,
    drift_ref,
    chosen,
    blocks,
    x_out,
    sum_out,
    anchor_out,
    omega_out,
    message,
    extrap,
    found,
):
    n = cost.shape[0]
    omega = omega_ref[0:1, :]
    if 1 <= k <= ITERS - 2:
        drift_x = drift_ref[0:1, :] / total_cols + epsilon
        drift_y = (here[n : n + 1, :] + there[n : n + 1, :]) / total_rows + epsilon
        later = jnp.sqrt(omega) * jnp.sqrt(jnp.sqrt(drift_x / drift_y))
        omega = jnp.where(restart[k - 1] == 1, later, omega)
    omega_out[...] = jnp.broadcast_to(omega, omega_out.shape)
    step_primal = step_scale / omega
    dual_image = here[0:n, :] + there[0:n, :]
    x = x_ref[...]
    x_next = jnp.minimum(
        jnp.maximum(x - step_primal * (cost[...] - dual_image), 0.0), bound[...]
    )
    extrap[...] = 2.0 * x_next - x
    extra = jnp.zeros((16, 256), f32)
    if k <= ITERS - 3:
        is_restart = restart[k] == 1
        summed = sum_ref[...] + x_next
        mean = summed / taken_by(restart, k)
        gap = mean - anchor_ref[...]
        extra = in_rows(jnp.sum(gap * gap), 0)
        x_out[...] = jnp.where(is_restart, mean, x_next)
        anchor_out[...] = jnp.where(is_restart, mean, anchor_ref[...])
        sum_out[...] = jnp.where(is_restart, 0.0, summed)
    else:
        x_out[...] = x_next
        sum_out[...] = jnp.zeros_like(sum_out)
        anchor_out[...] = jnp.zeros_like(anchor_out)
    products(cols, extrap, blocks, found, 1)
    values = found[...]
    high = values.astype(bf16)
    rest = values - high.astype(f32)
    middle = rest.astype(bf16)
    low = (rest - middle.astype(f32)).astype(bf16)
    picked = chosen[...]
    image = (
        jnp.dot(picked, low, preferred_element_type=f32)
        + jnp.dot(picked, middle, preferred_element_type=f32)
        + jnp.dot(picked, high, preferred_element_type=f32)
    )
    message[0 : image.shape[0], :] = image.astype(bf16)
    message[image.shape[0] :, :] = extra.astype(bf16)


def dual_step(
    k,
    restart,
    rows,
    live,
    own,
    before,
    opposite,
    after,
    demand,
    omega_ref,
    y_ref,
    sum_ref,
    anchor_ref,
    blocks,
    y_out,
    sum_out,
    anchor_out,
    drift_out,
    message,
    found,
):
    n = demand.shape[0]
    step_dual = step_scale * omega_ref[0:1, :]
    both = (own[...].astype(f32) + opposite[...].astype(f32)) + (
        before[...].astype(f32) + after[...].astype(f32)
    )
    image, tail = both[0:n, :], both[n:, :]
    drift_out[...] = jnp.broadcast_to(tail[0:1, :] + tail[1:2, :] + tail[2:3, :], (8, 256))
    y_next = jnp.maximum(y_ref[...] + step_dual * (demand[...] - image), 0.0)
    extra = jnp.zeros((16, 256), f32)
    if k <= ITERS - 3:
        is_restart = restart[k] == 1
        summed = sum_ref[...] + y_next
        mean = summed / taken_by(restart, k)
        gap = mean - anchor_ref[...]
        extra = in_rows(jnp.sum(gap * gap), 1)
        y_out[...] = jnp.where(is_restart, mean, y_next)
        anchor_out[...] = jnp.where(is_restart, mean, anchor_ref[...])
        sum_out[...] = jnp.where(is_restart, 0.0, summed)
    else:
        y_out[...] = y_next
        sum_out[...] = jnp.zeros_like(sum_out)
        anchor_out[...] = jnp.zeros_like(anchor_out)
    products(rows, y_out, blocks, found, 0)
    to_peers(live, found, extra, message)


def last_dual_step(own, before, opposite, after, demand, omega_ref, y_ref, y_out):
    n = demand.shape[0]
    step_dual = step_scale * omega_ref[0:1, :]
    image = (own[0:n, :].astype(f32) + opposite[0:n, :].astype(f32)) + (
        before[0:n, :].astype(f32) + after[0:n, :].astype(f32)
    )
    y_out[...] = jnp.maximum(y_ref[...] + step_dual * (demand[...] - image), 0.0)


def shards(
    block_values,
    block_rows,
    block_cols,
    live_count,
    objective,
    upper_bound,
    demand,
    primal_start,
    dual_start,
    restart_at,
):
    blocks = block_values[0, 0]
    rows = block_rows[0, 0]
    cols = block_cols[0, 0]
    live = live_count[0]
    slots, size = blocks.shape[0], blocks.shape[1]
    peers = lax.axis_size(XY)
    depth = lax.axis_size("col")
    total_cols = objective.shape[0] * depth
    total_rows = demand.shape[0] * lax.axis_size(ROW)
    cost = objective.reshape(-1, size)
    bound = upper_bound.reshape(-1, size)
    want = demand.reshape(-1, size)
    x = primal_start.reshape(-1, size)
    y = dual_start.reshape(-1, size)
    n_rows, n_cols = want.shape[0], cost.shape[0]
    live_slot = jnp.arange(slots, dtype=jnp.int32) < live[0]
    chosen_rows = (
        (rows[None, :] == jnp.arange(n_rows, dtype=jnp.int32)[:, None]) & live_slot[None, :]
    ).astype(bf16)
    cols_row = jnp.broadcast_to(
        jnp.pad(cols.astype(f32), (0, size - slots))[None, :], (8, size)
    )
    big, small = (n_cols, size), (n_rows, size)
    anchor_x, anchor_y = x, y
    sum_x, sum_y = jnp.zeros(big, f32), jnp.zeros(small, f32)
    omega = jnp.ones((8, size), f32)
    drift = jnp.zeros((8, size), f32)
    found = ((slots, size), f32)
    to_all = ((peers, MESSAGE_ROWS, size), bf16)
    work = 2 * slots * size * size * 8
    (message,) = call(
        first_dual, "first_dual", (rows, live), (cols_row, y, blocks), (to_all,), (found,), work
    )
    chosen_cols = None
    for k in range(ITERS):
        arrived = lax.all_to_all(message, XY, 0, 0, tiled=True)
        if k == 0:
            told = arrived[:, slots, :slots].astype(f32)
            told = jnp.pad(told, ((0, 0), (0, MESSAGE_ROWS - slots)), constant_values=-1.0)
            told = told.reshape(1, -1)
            chosen_cols = (
                told == lax.broadcasted_iota(jnp.int32, (n_cols, told.shape[1]), 0).astype(f32)
            ).astype(bf16)
        (here,) = call(
            sum_columns,
            f"sum_columns_{k}",
            (),
            (chosen_cols, arrived.reshape(-1, size)),
            (((n_cols + 8, size), f32),),
        )
        there = lax.ppermute(here, CORE, [(0, 1), (1, 0)])
        x, sum_x, anchor_x, omega, part = call(
            functools.partial(primal_step, k, total_cols, total_rows),
            f"primal_step_{k}",
            (restart_at, cols),
            (here, there, cost, bound, x, sum_x, anchor_x, omega, drift, chosen_rows, blocks),
            ((big, f32), (big, f32), (big, f32), ((8, size), f32), ((MESSAGE_ROWS, size), bf16)),
            ((big, f32), found),
            work,
        )
        after, before, opposite = (
            lax.ppermute(part, "col", [(i, (i + d) % depth) for i in range(depth)])
            for d in (1, 3, 2)
        )
        if k == ITERS - 1:
            (y,) = call(
                last_dual_step,
                "last_dual_step",
                (),
                (part, before, opposite, after, want, omega, y),
                ((small, f32),),
            )
        else:
            y, sum_y, anchor_y, drift, message = call(
                functools.partial(dual_step, k),
                f"dual_step_{k}",
                (restart_at, rows, live),
                (part, before, opposite, after, want, omega, y, sum_y, anchor_y, blocks),
                ((small, f32), (small, f32), (small, f32), ((8, size), f32), to_all),
                (found,),
                work,
            )
    return (x.reshape(-1), y.reshape(-1))


def solution(mesh):
    torus = Mesh(
        mesh.devices.reshape(4, 4, 2, mesh.shape["col"]), ("row_0", "row_1", "row_2", "col")
    )
    return jax.shard_map(
        shards,
        mesh=torus,
        in_specs=(
            P(ROW, "col", None, None, None),
            P(ROW, "col", None),
            P(ROW, "col", None),
            P(ROW, "col"),
            P("col"),
            P("col"),
            P(ROW),
            P("col"),
            P(ROW),
            P(),
        ),
        out_specs=(P("col"), P(ROW)),
        check_vma=False,
    )
```

```python
import functools

import jax
import jax.numpy as jnp
from jax import lax
from jax.experimental import pallas as pl
from jax.experimental.pallas import tpu as pltpu
from jax.sharding import Mesh
from jax.sharding import PartitionSpec as P

ITERS = 8
XY = ("row_0", "row_1")
CORE = "row_2"
ROW = ("row_0", "row_1", "row_2")
HALF = 128
CHUNK = 8

step_scale = 0.3
epsilon = 1e-06

f32, bf16 = jnp.float32, jnp.bfloat16
SCALARS = pl.BlockSpec(memory_space=pltpu.SMEM)
VECTORS = pl.BlockSpec(memory_space=pltpu.VMEM)
OUTSIDE = pl.BlockSpec(memory_space=pltpu.HBM)


def call(body, name, scalars, arrays, outs, scratch=(), flops=0, outside=(), kept=0, semaphores=0):
    moved = sum(a.size * a.dtype.itemsize for a in arrays)
    return pl.pallas_call(
        body,
        name=name,
        in_specs=[SCALARS] * len(scalars) + [VECTORS] * len(arrays) + [OUTSIDE] * len(outside),
        out_specs=[VECTORS] * len(outs),
        out_shape=[
            pltpu.VMEM(s, t) if i < kept else jax.ShapeDtypeStruct(s, t)
            for i, (s, t) in enumerate(outs)
        ],
        scratch_shapes=[pltpu.VMEM(s, t) for s, t in scratch]
        + [pltpu.SemaphoreType.DMA((semaphores,))] * (semaphores > 0),
        compiler_params=pltpu.CompilerParams(vmem_limit_bytes=24 << 20),
        cost_estimate=pl.CostEstimate(flops=flops, bytes_accessed=moved, transcendentals=0),
    )(*scalars, *arrays, *outside)


def products(index, source, blocks, target, first=0, count=None):
    def step(t, carry):
        piece = source[pl.ds(index[t], 1), :].astype(bf16)
        target[pl.ds(t, 1), :] = jnp.dot(piece, blocks[t], preferred_element_type=f32)
        return carry

    count = blocks.shape[0] if count is None else count
    lax.fori_loop(first, first + count, step, 0, unroll=True)


def in_rows(total, first):
    row = lax.broadcasted_iota(jnp.int32, (16, HALF), 0)
    whole = jnp.full((16, HALF), total, f32)
    high = whole.astype(bf16).astype(f32)
    middle = (whole - high).astype(bf16).astype(f32)
    low = whole - high - middle
    zero = jnp.zeros_like(whole)
    return jnp.where(
        row == first,
        high,
        jnp.where(row == first + 1, middle, jnp.where(row == first + 2, low, zero)),
    )


def taken_by(restart, k):
    taken = jnp.int32(1)
    for j in range(k):
        taken = jnp.where(restart[j] == 1, 1, taken + 1)
    return taken.astype(f32)


def pack(values, extra):
    return jnp.concatenate(
        [values[:, :HALF].astype(bf16), values[:, HALF:].astype(bf16), extra.astype(bf16)], axis=0
    )


def to_peers(live, found, extra, message):
    slot = lax.broadcasted_iota(jnp.int32, found.shape, 0)
    packed = pack(jnp.where(slot < live[0], found[...], 0.0), extra)
    for p in range(message.shape[0]):
        message[p] = packed


def first_dual(rows, live, cols_row, y, stored, blocks, message, found, arrivals):
    copies = [
        pltpu.make_async_copy(
            stored.at[pl.ds(c * CHUNK, CHUNK)], blocks.at[pl.ds(c * CHUNK, CHUNK)], arrivals.at[c]
        )
        for c in range(blocks.shape[0] // CHUNK)
    ]
    for copy in copies:
        copy.start()
    for c, copy in enumerate(copies):
        copy.wait()
        products(rows, y, blocks, found, c * CHUNK, CHUNK)
    row = lax.broadcasted_iota(jnp.int32, (16, HALF), 0)
    extra = jnp.where(row == 0, jnp.broadcast_to(cols_row[0:1, :], (16, HALF)), 0.0)
    to_peers(live, found, extra, message)


def turn(blocks, turned):
    def step(t, carry):
        turned[t] = blocks[t].T
        return carry

    lax.fori_loop(0, blocks.shape[0], step, 0, unroll=4)


def sum_columns(chosen, arrived, half, lined):
    n = chosen.shape[0]
    peers = arrived.shape[0]
    slots = lined.shape[0] // peers
    tail = jnp.zeros((16, HALF), f32)
    for p in range(peers):
        lined[p * slots : (p + 1) * slots, :HALF] = arrived[p, :slots, :]
        lined[p * slots : (p + 1) * slots, HALF:] = arrived[p, slots : 2 * slots, :]
        tail = tail + arrived[p, 2 * slots :, :].astype(f32)
    half[0:n, :] = jnp.dot(chosen[...], lined[...], preferred_element_type=f32)
    total = tail[1:2, :] + tail[2:3, :] + tail[3:4, :]
    total = jnp.broadcast_to(total, (8, HALF))
    half[n : n + 8, :] = jnp.concatenate([total, total], axis=1)


def primal_step(
    k,
    total_cols,
    total_rows,
    restart,
    cols,
    here,
    there,
    cost,
    bound,
    x_ref,
    sum_ref,
    anchor_ref,
    omega_ref,
    drift_ref,
    chosen,
    blocks,
    x_out,
    sum_out,
    anchor_out,
    omega_out,
    message,
    extrap,
    found,
):
    n = cost.shape[0]
    omega = omega_ref[0:1, :]
    if 1 <= k <= ITERS - 2:
        drift_x = drift_ref[0:1, :] / total_cols + epsilon
        drift_y = (here[n : n + 1, :] + there[n : n + 1, :]) / total_rows + epsilon
        later = jnp.sqrt(omega) * jnp.sqrt(jnp.sqrt(drift_x / drift_y))
        omega = jnp.where(restart[k - 1] == 1, later, omega)
    omega_out[...] = jnp.broadcast_to(omega, omega_out.shape)
    step_primal = step_scale / omega
    dual_image = here[0:n, :] + there[0:n, :]
    x = x_ref[...]
    x_next = jnp.minimum(
        jnp.maximum(x - step_primal * (cost[...] - dual_image), 0.0), bound[...]
    )
    extrap[...] = 2.0 * x_next - x
    extra = jnp.zeros((16, HALF), f32)
    if k <= ITERS - 3:
        is_restart = restart[k] == 1
        summed = sum_ref[...] + x_next
        mean = summed / taken_by(restart, k)
        gap = mean - anchor_ref[...]
        extra = in_rows(jnp.sum(gap * gap), 0)
        x_out[...] = jnp.where(is_restart, mean, x_next)
        anchor_out[...] = jnp.where(is_restart, mean, anchor_ref[...])
        sum_out[...] = jnp.where(is_restart, 0.0, summed)
    else:
        x_out[...] = x_next
        sum_out[...] = jnp.zeros_like(sum_out)
        anchor_out[...] = jnp.zeros_like(anchor_out)
    products(cols, extrap, blocks, found)
    values = found[...]
    high = values.astype(bf16)
    rest = values - high.astype(f32)
    middle = rest.astype(bf16)
    low = (rest - middle.astype(f32)).astype(bf16)
    picked = chosen[...]
    image = (
        jnp.dot(picked, low, preferred_element_type=f32)
        + jnp.dot(picked, middle, preferred_element_type=f32)
        + jnp.dot(picked, high, preferred_element_type=f32)
    )
    message[...] = pack(image, extra)


def summed_image(n, own, before, opposite, after):
    both = (own[...].astype(f32) + opposite[...].astype(f32)) + (
        before[...].astype(f32) + after[...].astype(f32)
    )
    return jnp.concatenate([both[0:n, :], both[n : 2 * n, :]], axis=1), both[2 * n :, :]


def dual_step(
    k,
    restart,
    rows,
    live,
    own,
    before,
    opposite,
    after,
    demand,
    omega_ref,
    y_ref,
    sum_ref,
    anchor_ref,
    blocks,
    y_out,
    sum_out,
    anchor_out,
    drift_out,
    message,
    found,
):
    n = demand.shape[0]
    step_dual = step_scale * omega_ref[0:1, :]
    image, tail = summed_image(n, own, before, opposite, after)
    tail = jnp.broadcast_to(tail[0:1, :] + tail[1:2, :] + tail[2:3, :], (8, HALF))
    drift_out[...] = jnp.concatenate([tail, tail], axis=1)
    y_next = jnp.maximum(y_ref[...] + step_dual * (demand[...] - image), 0.0)
    extra = jnp.zeros((16, HALF), f32)
    if k <= ITERS - 3:
        is_restart = restart[k] == 1
        summed = sum_ref[...] + y_next
        mean = summed / taken_by(restart, k)
        gap = mean - anchor_ref[...]
        extra = in_rows(jnp.sum(gap * gap), 1)
        y_out[...] = jnp.where(is_restart, mean, y_next)
        anchor_out[...] = jnp.where(is_restart, mean, anchor_ref[...])
        sum_out[...] = jnp.where(is_restart, 0.0, summed)
    else:
        y_out[...] = y_next
        sum_out[...] = jnp.zeros_like(sum_out)
        anchor_out[...] = jnp.zeros_like(anchor_out)
    products(rows, y_out, blocks, found)
    to_peers(live, found, extra, message)


def last_dual_step(own, before, opposite, after, demand, omega_ref, y_ref, y_out):
    n = demand.shape[0]
    step_dual = step_scale * omega_ref[0:1, :]
    image, unused = summed_image(n, own, before, opposite, after)
    y_out[...] = jnp.maximum(y_ref[...] + step_dual * (demand[...] - image), 0.0)


def shards(
    block_values,
    block_rows,
    block_cols,
    live_count,
    objective,
    upper_bound,
    demand,
    primal_start,
    dual_start,
    restart_at,
):
    blocks = block_values[0, 0]
    rows = block_rows[0, 0]
    cols = block_cols[0, 0]
    live = live_count[0]
    slots, size = blocks.shape[0], blocks.shape[1]
    peers = lax.axis_size(XY)
    depth = lax.axis_size("col")
    total_cols = objective.shape[0] * depth
    total_rows = demand.shape[0] * lax.axis_size(ROW)
    cost = objective.reshape(-1, size)
    bound = upper_bound.reshape(-1, size)
    want = demand.reshape(-1, size)
    x = primal_start.reshape(-1, size)
    y = dual_start.reshape(-1, size)
    n_rows, n_cols = want.shape[0], cost.shape[0]
    live_slot = jnp.arange(slots, dtype=jnp.int32) < live[0]
    chosen_rows = (
        (rows[None, :] == jnp.arange(n_rows, dtype=jnp.int32)[:, None]) & live_slot[None, :]
    ).astype(bf16)
    cols_row = jnp.broadcast_to(
        jnp.pad(cols.astype(f32), (0, HALF - slots))[None, :], (8, HALF)
    )
    big, small = (n_cols, size), (n_rows, size)
    anchor_x, anchor_y = x, y
    sum_x, sum_y = jnp.zeros(big, f32), jnp.zeros(small, f32)
    omega = jnp.ones((8, size), f32)
    drift = jnp.zeros((8, size), f32)
    found = ((slots, size), f32)
    to_all = ((peers, 2 * slots + 16, HALF), bf16)
    to_column = ((2 * n_rows + 16, HALF), bf16)
    held = ((slots, size, size), bf16)
    work = 2 * slots * size * size * 8
    blocks, message = call(
        first_dual,
        "first_dual",
        (rows, live),
        (cols_row, y),
        (held, to_all),
        (found,),
        work,
        (blocks,),
        1,
        slots // CHUNK,
    )
    blocks = pltpu.with_memory_space_constraint(blocks, pltpu.VMEM)
    (turned,) = call(turn, "turn", (), (blocks,), (held,), kept=1)
    turned = pltpu.with_memory_space_constraint(turned, pltpu.VMEM)
    chosen_cols = None
    for k in range(ITERS):
        arrived = lax.all_to_all(message, XY, 0, 0, tiled=True)
        if k == 0:
            told = arrived[:, 2 * slots, :slots].astype(f32).reshape(1, -1)
            chosen_cols = (
                told == lax.broadcasted_iota(jnp.int32, (n_cols, told.shape[1]), 0).astype(f32)
            ).astype(bf16)
        (here,) = call(
            sum_columns,
            f"sum_columns_{k}",
            (),
            (chosen_cols, arrived),
            (((n_cols + 8, size), f32),),
            (((peers * slots, size), bf16),),
        )
        there = lax.ppermute(here, CORE, [(0, 1), (1, 0)])
        x, sum_x, anchor_x, omega, part = call(
            functools.partial(primal_step, k, total_cols, total_rows),
            f"primal_step_{k}",
            (restart_at, cols),
            (here, there, cost, bound, x, sum_x, anchor_x, omega, drift, chosen_rows, turned),
            ((big, f32), (big, f32), (big, f32), ((8, size), f32), to_column),
            ((big, f32), found),
            work,
        )
        after, before, opposite = (
            lax.ppermute(part, "col", [(i, (i + d) % depth) for i in range(depth)])
            for d in (1, 3, 2)
        )
        if k == ITERS - 1:
            (y,) = call(
                last_dual_step,
                "last_dual_step",
                (),
                (part, before, opposite, after, want, omega, y),
                ((small, f32),),
            )
        else:
            y, sum_y, anchor_y, drift, message = call(
                functools.partial(dual_step, k),
                f"dual_step_{k}",
                (restart_at, rows, live),
                (part, before, opposite, after, want, omega, y, sum_y, anchor_y, blocks),
                ((small, f32), (small, f32), (small, f32), ((8, size), f32), to_all),
                (found,),
                work,
            )
    return (x.reshape(-1), y.reshape(-1))


def solution(mesh):
    torus = Mesh(
        mesh.devices.reshape(4, 4, 2, mesh.shape["col"]), ("row_0", "row_1", "row_2", "col")
    )
    return jax.shard_map(
        shards,
        mesh=torus,
        in_specs=(
            P(ROW, "col", None, None, None),
            P(ROW, "col", None),
            P(ROW, "col", None),
            P(ROW, "col"),
            P("col"),
            P("col"),
            P(ROW),
            P("col"),
            P(ROW),
            P(),
        ),
        out_specs=(P("col"), P(ROW)),
        check_vma=False,
    )
```

```python
import functools
import types

import jax
import jax.numpy as jnp
from jax import lax
from jax.experimental import pallas as pl
from jax.experimental.pallas import tpu as pltpu
from jax.sharding import Mesh
from jax.sharding import PartitionSpec as P

ITERS = 8
XY = ("row_0", "row_1")
CORE = "row_2"
ROW = ("row_0", "row_1", "row_2")
HALF = 128
CHUNK = 8
LAST_RESTART = ITERS - 3

step_scale = 0.3
epsilon = 1e-06

f32, bf16 = jnp.float32, jnp.bfloat16


def call(body, name, scalars, arrays, outs, scratch, outside=(), held=(), flops=0):
    names = [*scalars, *arrays, *outs, *scratch]

    def run(*refs):
        body(types.SimpleNamespace(**dict(zip(names, refs, strict=True))))

    def spec(key):
        return pl.BlockSpec(memory_space=pltpu.HBM if key in outside else pltpu.VMEM)

    def placed(key, array):
        space = pltpu.HBM if key in outside else pltpu.VMEM
        return pltpu.with_memory_space_constraint(array, space) if key in (*outside, *held) else array

    results = pl.pallas_call(
        run,
        name=name,
        in_specs=[pl.BlockSpec(memory_space=pltpu.SMEM)] * len(scalars) + [spec(k) for k in arrays],
        out_specs=[spec(k) for k in outs],
        out_shape=[
            pltpu.VMEM(*o) if k in held else jax.ShapeDtypeStruct(*o) for k, o in outs.items()
        ],
        scratch_shapes=list(scratch.values()),
        compiler_params=pltpu.CompilerParams(vmem_limit_bytes=24 << 20),
        cost_estimate=pl.CostEstimate(flops=flops, bytes_accessed=flops // 8, transcendentals=0),
    )(*scalars.values(), *(placed(k, a) for k, a in arrays.items()))
    return dict(zip(outs, results, strict=True))


def split_halves(ref, values):
    n = values.shape[0]
    ref[pl.ds(0, n, stride=2), :] = values[:, :HALF]
    ref[pl.ds(1, n, stride=2), :] = values[:, HALF:]


def products(index, source, blocks, target, base=0, first=0, count=None):
    def step(t, carry):
        at = 2 * index[t]
        piece = jnp.concatenate([source[pl.ds(at, 1), :], source[pl.ds(at + 1, 1), :]], axis=1)
        target[pl.ds(t, 1), :] = jnp.dot(
            piece.astype(bf16), blocks[base + t], preferred_element_type=f32
        )
        return carry

    count = target.shape[0] if count is None else count
    lax.fori_loop(first, first + count, step, 0, unroll=True)


def in_rows(total, first):
    row = lax.broadcasted_iota(jnp.int32, (16, HALF), 0)
    whole = jnp.full((16, HALF), total, f32)
    high = whole.astype(bf16).astype(f32)
    middle = (whole - high).astype(bf16).astype(f32)
    low = whole - high - middle
    zero = jnp.zeros_like(whole)
    return jnp.where(
        row == first,
        high,
        jnp.where(row == first + 1, middle, jnp.where(row == first + 2, low, zero)),
    )


def taken_by(restart, k):
    taken = jnp.int32(1)
    for j in range(k):
        taken = jnp.where(restart[j] == 1, 1, taken + 1)
    return taken.astype(f32)


def pack(values, extra):
    return jnp.concatenate(
        [values[:, :HALF].astype(bf16), values[:, HALF:].astype(bf16), extra.astype(bf16)], axis=0
    )


def to_peers(live, found, extra, message):
    slot = lax.broadcasted_iota(jnp.int32, found.shape, 0)
    packed = pack(jnp.where(slot < live[0], found[...], 0.0), extra)
    for p in range(message.shape[0]):
        message[p] = packed


def average(r, k, new, old, now, row):
    if k > LAST_RESTART:
        now[...] = new
        return jnp.zeros((16, HALF), f32)
    is_restart = r.restart[k] == 1
    summed, anchor = (new, old) if k == 0 else (r.sum[...] + new, r.anchor[...])
    mean = summed / taken_by(r.restart, k)
    gap = mean - anchor
    now[...] = jnp.where(is_restart, mean, new)
    r.anchor_out[...] = jnp.where(is_restart, mean, anchor)
    r.sum_out[...] = jnp.where(is_restart, 0.0, summed)
    return in_rows(jnp.sum(gap * gap), row)


def first_dual(r):
    slots = r.stored.shape[0]
    copies = [
        pltpu.make_async_copy(
            r.stored.at[pl.ds(c * CHUNK, CHUNK)],
            r.blocks.at[pl.ds(c * CHUNK, CHUNK)],
            r.arrivals.at[c],
        )
        for c in range(slots // CHUNK)
    ]
    for copy in copies:
        copy.start()
    here = jnp.broadcast_to(r.index[1:2, :slots], r.picked.shape)
    row = lax.broadcasted_iota(jnp.int32, r.picked.shape, 0)
    slot = lax.broadcasted_iota(jnp.int32, r.picked.shape, 1)
    r.picked[...] = jnp.where((here == row) & (slot < r.live[0]), 1.0, 0.0).astype(bf16)
    for c, copy in enumerate(copies):
        copy.wait()
        products(r.rows, r.y, r.blocks, r.found, 0, c * CHUNK, CHUNK)
        for t in range(c * CHUNK, (c + 1) * CHUNK):
            r.blocks[slots + t] = r.blocks[t].T
    row = lax.broadcasted_iota(jnp.int32, (16, HALF), 0)
    told = jnp.broadcast_to(r.index[0:1, :].astype(f32), (16, HALF))
    to_peers(r.live, r.found, jnp.where(row == 0, told, 0.0), r.message)


def sum_columns(k, r):
    peers = r.arrived.shape[0]
    slots = r.lined.shape[0] // peers
    chosen = r.told if k == 0 else r.chosen
    tail = jnp.zeros((16, HALF), f32)
    for p in range(peers):
        r.lined[p * slots : (p + 1) * slots, :HALF] = r.arrived[p, :slots, :]
        r.lined[p * slots : (p + 1) * slots, HALF:] = r.arrived[p, slots : 2 * slots, :]
        tail = tail + r.arrived[p, 2 * slots :, :].astype(f32)
    if k == 0:
        shape = (chosen.shape[0], HALF)
        block = lax.broadcasted_iota(jnp.int32, shape, 0).astype(f32)
        early = lax.broadcasted_iota(jnp.int32, (1, HALF), 1) < slots
        for p in range(0, peers, 2):
            pair = [r.arrived[q, 2 * slots :, :].astype(f32)[0:1, :] for q in (p, p + 1)]
            told = jnp.broadcast_to(jnp.where(early, pair[0], pair[1]), shape)
            chosen[:, p * slots : (p + 2) * slots] = jnp.where(told == block, 1.0, 0.0).astype(bf16)
    n = chosen.shape[0]
    split_halves(r.half, jnp.dot(chosen[...], r.lined[...], preferred_element_type=f32))
    total = tail[1:2, :] + tail[2:3, :] + tail[3:4, :]
    r.half[2 * n : 2 * n + 8, :] = jnp.broadcast_to(total, (8, HALF))


def primal_step(k, total_cols, total_rows, r):
    n = r.cost.shape[0]
    omega = jnp.ones((1, HALF), f32) if k == 0 else r.omega[0:1, :]
    if 1 <= k <= LAST_RESTART + 1:
        drift_x = r.drift[0:1, :] / total_cols + epsilon
        drift_y = (r.here[n : n + 1, :] + r.there[n : n + 1, :]) / total_rows + epsilon
        later = jnp.sqrt(omega) * jnp.sqrt(jnp.sqrt(drift_x / drift_y))
        omega = jnp.where(r.restart[k - 1] == 1, later, omega)
    r.omega_out[...] = jnp.broadcast_to(omega, r.omega_out.shape)
    step_primal = step_scale / omega
    dual_image = r.here[0:n, :] + r.there[0:n, :]
    x = r.x[...]
    x_next = jnp.minimum(
        jnp.maximum(x - step_primal * (r.cost[...] - dual_image), 0.0), r.bound[...]
    )
    r.extrap[...] = 2.0 * x_next - x
    extra = average(r, k, x_next, x, r.x_out, 0)
    products(r.cols, r.extrap, r.blocks, r.found, r.found.shape[0])
    values = r.found[...]
    high = values.astype(bf16)
    rest = values - high.astype(f32)
    middle = rest.astype(bf16)
    low = (rest - middle.astype(f32)).astype(bf16)
    picked = r.picked[...]
    image = (
        jnp.dot(picked, low, preferred_element_type=f32)
        + jnp.dot(picked, middle, preferred_element_type=f32)
        + jnp.dot(picked, high, preferred_element_type=f32)
    )
    r.message[...] = pack(image, extra)


def dual_step(k, r):
    n = r.demand.shape[0] // 2
    step_dual = step_scale * r.omega[0:1, :]
    both = (r.own[...].astype(f32) + r.opposite[...].astype(f32)) + (
        r.before[...].astype(f32) + r.after[...].astype(f32)
    )
    r.image[pl.ds(0, n, stride=2), :] = both[0:n, :]
    r.image[pl.ds(1, n, stride=2), :] = both[n : 2 * n, :]
    y = r.y[...]
    y_next = jnp.maximum(y + step_dual * (r.demand[...] - r.image[...]), 0.0)
    if k == ITERS - 1:
        r.y_out[...] = y_next
        return
    tail = both[2 * n :, :]
    r.drift_out[...] = jnp.broadcast_to(tail[0:1, :] + tail[1:2, :] + tail[2:3, :], (8, HALF))
    extra = average(r, k, y_next, y, r.y_out, 1)
    products(r.rows, r.y_out, r.blocks, r.found)
    to_peers(r.live, r.found, extra, r.message)


def shards(
    block_values,
    block_rows,
    block_cols,
    live_count,
    objective,
    upper_bound,
    demand,
    primal_start,
    dual_start,
    restart_at,
):
    blocks = block_values[0, 0]
    rows = block_rows[0, 0]
    cols = block_cols[0, 0]
    live = live_count[0]
    slots, size = blocks.shape[0], blocks.shape[1]
    peers = lax.axis_size(XY)
    depth = lax.axis_size("col")
    total_cols = objective.shape[0] * depth
    total_rows = demand.shape[0] * lax.axis_size(ROW)
    cost, bound, want, x, y = (
        v.reshape(-1, HALF) for v in (objective, upper_bound, demand, primal_start, dual_start)
    )
    n_rows, n_cols = demand.shape[0] // size, objective.shape[0] // size
    big, small, one = (cost.shape, f32), (want.shape, f32), ((8, HALF), f32)
    to_all = ((peers, 2 * slots + 16, HALF), bf16)
    to_column = ((2 * n_rows + 16, HALF), bf16)
    half = ((2 * n_cols + 8, HALF), f32)
    chosen = ((n_cols, peers * slots), bf16)
    found = pltpu.VMEM((slots, size), f32)
    work = 2 * slots * size * size * 8
    index = jnp.stack([jnp.concatenate([cols, cols]), jnp.concatenate([rows, rows])])
    made = call(
        first_dual,
        "first_dual",
        {"rows": rows, "live": live},
        {"index": index, "y": y, "stored": blocks},
        {
            "blocks": ((2 * slots, size, size), bf16),
            "message": to_all,
            "picked": ((n_rows, slots), bf16),
        },
        {"found": found, "arrivals": pltpu.SemaphoreType.DMA((slots // CHUNK,))},
        ("stored",),
        ("blocks",),
        work,
    )
    blocks, message, picked = made["blocks"], made["message"], made["picked"]
    state_x, state_y, omega, drift, told = {}, {}, {}, {}, {}
    for k in range(ITERS):
        arrived = lax.all_to_all(message, XY, 0, 0, tiled=True)
        made = call(
            functools.partial(sum_columns, k),
            f"sum_columns_{k}",
            {},
            {"arrived": arrived} | told,
            {"half": half} | ({"told": chosen} if k == 0 else {}),
            {"lined": pltpu.VMEM((peers * slots, size), bf16)},
        )
        here = made["half"]
        if k == 0:
            told = {"chosen": made["told"]}
        there = lax.ppermute(here, CORE, [(0, 1), (1, 0)])
        averaged = k <= LAST_RESTART
        sums = ("sum_out", "anchor_out") if averaged else ()
        if not averaged:
            state_x, state_y = {}, {}
        made = call(
            functools.partial(primal_step, k, total_cols, total_rows),
            f"primal_step_{k}",
            {"restart": restart_at, "cols": cols},
            {"here": here, "there": there, "cost": cost, "bound": bound, "x": x}
            | state_x
            | omega
            | drift
            | {"picked": picked, "blocks": blocks},
            {"x_out": big, "omega_out": one, "message": to_column} | dict.fromkeys(sums, big),
            {"extrap": pltpu.VMEM(*big), "found": found},
            held=("blocks",),
            flops=work,
        )
        x, part, omega = made["x_out"], made["message"], {"omega": made["omega_out"]}
        if averaged:
            state_x = {"sum": made["sum_out"], "anchor": made["anchor_out"]}
        after, before, opposite = (
            lax.ppermute(part, "col", [(i, (i + d) % depth) for i in range(depth)])
            for d in (1, 3, 2)
        )
        parts = {"own": part, "before": before, "opposite": opposite, "after": after}
        image = {"image": pltpu.VMEM(*small)}
        if k == ITERS - 1:
            made = call(
                functools.partial(dual_step, k),
                f"dual_step_{k}",
                {},
                parts | {"demand": want, "y": y} | omega,
                {"y_out": small},
                image,
            )
            y = made["y_out"]
        else:
            made = call(
                functools.partial(dual_step, k),
                f"dual_step_{k}",
                {"restart": restart_at, "rows": rows, "live": live},
                parts | {"demand": want, "y": y} | omega | state_y | {"blocks": blocks},
                {"y_out": small, "drift_out": one, "message": to_all} | dict.fromkeys(sums, small),
                image | {"found": found},
                held=("blocks",),
                flops=work,
            )
            y, message, drift = made["y_out"], made["message"], {"drift": made["drift_out"]}
            if averaged:
                state_y = {"sum": made["sum_out"], "anchor": made["anchor_out"]}
    return (x.reshape(-1), y.reshape(-1))


def solution(mesh):
    torus = Mesh(
        mesh.devices.reshape(4, 4, 2, mesh.shape["col"]), ("row_0", "row_1", "row_2", "col")
    )
    return jax.shard_map(
        shards,
        mesh=torus,
        in_specs=(
            P(ROW, "col", None, None, None),
            P(ROW, "col", None),
            P(ROW, "col", None),
            P(ROW, "col"),
            P("col"),
            P("col"),
            P(ROW),
            P("col"),
            P(ROW),
            P(),
        ),
        out_specs=(P("col"), P(ROW)),
        check_vma=False,
    )
```

```python
import functools
import types

import jax
import jax.numpy as jnp
from jax import lax
from jax.experimental import pallas as pl
from jax.experimental.pallas import tpu as pltpu
from jax.sharding import Mesh
from jax.sharding import PartitionSpec as P

ITERS = 8
XY = ("row_0", "row_1")
CORE = "row_2"
ROW = ("row_0", "row_1", "row_2")
HALF = 128
CHUNK = 8
UNROLL = 32
LAST_RESTART = ITERS - 3
AT_COLS, AT_ROWS, AT_LIVE, AT_RESTART = 0, 64, 128, 136

step_scale = 0.3
epsilon = 1e-06

f32, bf16 = jnp.float32, jnp.bfloat16
VECTORS = ("y", "demand", "cost", "bound", "x")


def call(body, name, scalars, arrays, outs, scratch, outside=(), held=(), flops=0):
    names = [*scalars, *arrays, *outs, *scratch]

    def run(*refs):
        body(types.SimpleNamespace(**dict(zip(names, refs, strict=True))))

    def spec(key):
        return pl.BlockSpec(memory_space=pltpu.HBM if key in outside else pltpu.VMEM)

    def placed(key, array):
        space = pltpu.HBM if key in outside else pltpu.VMEM
        return pltpu.with_memory_space_constraint(array, space) if key in (*outside, *held) else array

    results = pl.pallas_call(
        run,
        name=name,
        in_specs=[pl.BlockSpec(memory_space=pltpu.SMEM)] * len(scalars) + [spec(k) for k in arrays],
        out_specs=[spec(k) for k in outs],
        out_shape=[
            pltpu.VMEM(*o) if k in held else jax.ShapeDtypeStruct(*o) for k, o in outs.items()
        ],
        scratch_shapes=list(scratch.values()),
        compiler_params=pltpu.CompilerParams(vmem_limit_bytes=24 << 20),
        cost_estimate=pl.CostEstimate(flops=flops, bytes_accessed=flops // 8, transcendentals=0),
    )(*scalars.values(), *(placed(k, a) for k, a in arrays.items()))
    return dict(zip(outs, results, strict=True))


def split_halves(ref, values):
    n = values.shape[0]
    ref[pl.ds(0, n, stride=2), :] = values[:, :HALF]
    ref[pl.ds(1, n, stride=2), :] = values[:, HALF:]


def products(index, offset, source, blocks, target, base=0, first=0, count=None):
    def step(t, carry):
        at = 2 * index[offset + t]
        piece = jnp.concatenate([source[pl.ds(at, 1), :], source[pl.ds(at + 1, 1), :]], axis=1)
        target[pl.ds(t, 1), :] = jnp.dot(
            piece.astype(bf16), blocks[base + t], preferred_element_type=f32
        )
        return carry

    count = target.shape[0] if count is None else count
    lax.fori_loop(first, first + count, step, 0, unroll=min(count, UNROLL))


def in_rows(total, first):
    row = lax.broadcasted_iota(jnp.int32, (16, HALF), 0)
    whole = jnp.full((16, HALF), total, f32)
    high = whole.astype(bf16).astype(f32)
    middle = (whole - high).astype(bf16).astype(f32)
    low = whole - high - middle
    zero = jnp.zeros_like(whole)
    return jnp.where(
        row == first,
        high,
        jnp.where(row == first + 1, middle, jnp.where(row == first + 2, low, zero)),
    )


def restarts(r, j):
    return r.ints[AT_RESTART + j] == 1


def taken_by(r, k):
    taken = jnp.int32(1)
    for j in range(k):
        taken = jnp.where(restarts(r, j), 1, taken + 1)
    return taken.astype(f32)


def pack(values, extra):
    return jnp.concatenate(
        [values[:, :HALF].astype(bf16), values[:, HALF:].astype(bf16), extra.astype(bf16)], axis=0
    )


def to_peers(r, extra):
    slot = lax.broadcasted_iota(jnp.int32, r.found.shape, 0)
    packed = pack(jnp.where(slot < r.ints[AT_LIVE], r.found[...], 0.0), extra)
    for p in range(r.message.shape[0]):
        r.message[p] = packed


def average(r, k, new, old, now, row):
    if k > LAST_RESTART:
        now[...] = new
        return jnp.zeros((16, HALF), f32)
    is_restart = restarts(r, k)
    summed, anchor = (new, old) if k == 0 else (r.sum[...] + new, r.anchor[...])
    mean = summed / taken_by(r, k)
    gap = mean - anchor
    now[...] = jnp.where(is_restart, mean, new)
    if k < LAST_RESTART:
        r.anchor_out[...] = jnp.where(is_restart, mean, anchor)
        r.sum_out[...] = jnp.where(is_restart, 0.0, summed)
    return in_rows(jnp.sum(gap * gap), row)


def first_dual(r):
    slots = r.stored.shape[0]
    vectors = [
        pltpu.make_async_copy(getattr(r, v + "_stored"), getattr(r, v), r.vector_arrivals.at[i])
        for i, v in enumerate(VECTORS)
    ]
    copies = [
        pltpu.make_async_copy(
            r.stored.at[pl.ds(c * CHUNK, CHUNK)],
            r.blocks.at[pl.ds(c * CHUNK, CHUNK)],
            r.arrivals.at[c],
        )
        for c in range(slots // CHUNK)
    ]
    for copy in (vectors[0], *copies, *vectors[1:]):
        copy.start()
    cols_then_rows = jnp.broadcast_to(r.index[0:1, :], (16, HALF))
    here = pltpu.roll(cols_then_rows, HALF - slots, 1)[0:1, :slots]
    here = jnp.broadcast_to(here, r.picked.shape)
    row = lax.broadcasted_iota(jnp.int32, r.picked.shape, 0)
    slot = lax.broadcasted_iota(jnp.int32, r.picked.shape, 1)
    r.picked[...] = jnp.where((here == row) & (slot < r.ints[AT_LIVE]), 1.0, 0.0).astype(bf16)
    vectors[0].wait()
    for c, copy in enumerate(copies):
        copy.wait()
        products(r.ints, AT_ROWS, r.y, r.blocks, r.found, 0, c * CHUNK, CHUNK)
        for t in range(c * CHUNK, (c + 1) * CHUNK):
            r.blocks[slots + t] = r.blocks[t].T
    row = lax.broadcasted_iota(jnp.int32, (16, HALF), 0)
    to_peers(r, jnp.where(row == 0, cols_then_rows.astype(f32), 0.0))
    for copy in vectors[1:]:
        copy.wait()


def sum_columns(k, r):
    peers = r.arrived.shape[0]
    slots = r.lined.shape[0] // peers
    chosen = r.told if k == 0 else r.chosen
    tail = jnp.zeros((16, HALF), f32)
    for p in range(peers):
        r.lined[p * slots : (p + 1) * slots, :HALF] = r.arrived[p, :slots, :]
        r.lined[p * slots : (p + 1) * slots, HALF:] = r.arrived[p, slots : 2 * slots, :]
        tail = tail + r.arrived[p, 2 * slots :, :].astype(f32)
    if k == 0:
        shape = (chosen.shape[0], HALF)
        block = lax.broadcasted_iota(jnp.int32, shape, 0).astype(f32)
        early = lax.broadcasted_iota(jnp.int32, (1, HALF), 1) < slots
        for p in range(0, peers, 2):
            pair = [r.arrived[q, 2 * slots :, :].astype(f32) for q in (p, p + 1)]
            told = jnp.where(early, pair[0][0:1, :], pltpu.roll(pair[1], slots, 1)[0:1, :])
            told = jnp.broadcast_to(told, shape)
            chosen[:, p * slots : (p + 2) * slots] = jnp.where(told == block, 1.0, 0.0).astype(bf16)
    n = chosen.shape[0]
    split_halves(r.half, jnp.dot(chosen[...], r.lined[...], preferred_element_type=f32))
    total = tail[1:2, :] + tail[2:3, :] + tail[3:4, :]
    r.half[2 * n : 2 * n + 8, :] = jnp.broadcast_to(total, (8, HALF))


def primal_step(k, total_cols, total_rows, r):
    n = r.cost.shape[0]
    omega = jnp.ones((1, HALF), f32) if k == 0 else r.omega[0:1, :]
    if 1 <= k <= LAST_RESTART + 1:
        drift_x = r.drift[0:1, :] / total_cols + epsilon
        drift_y = (r.here[n : n + 1, :] + r.there[n : n + 1, :]) / total_rows + epsilon
        later = jnp.sqrt(omega) * jnp.sqrt(jnp.sqrt(drift_x / drift_y))
        omega = jnp.where(restarts(r, k - 1), later, omega)
    r.omega_out[...] = jnp.broadcast_to(omega, r.omega_out.shape)
    step_primal = step_scale / omega
    dual_image = r.here[0:n, :] + r.there[0:n, :]
    x = r.x[...]
    x_next = jnp.minimum(
        jnp.maximum(x - step_primal * (r.cost[...] - dual_image), 0.0), r.bound[...]
    )
    r.extrap[...] = 2.0 * x_next - x
    extra = average(r, k, x_next, x, r.x_out, 0)
    products(r.ints, AT_COLS, r.extrap, r.blocks, r.found, r.found.shape[0])
    values = r.found[...]
    high = values.astype(bf16)
    rest = values - high.astype(f32)
    middle = rest.astype(bf16)
    low = (rest - middle.astype(f32)).astype(bf16)
    picked = r.picked[...]
    image = (
        jnp.dot(picked, low, preferred_element_type=f32)
        + jnp.dot(picked, middle, preferred_element_type=f32)
        + jnp.dot(picked, high, preferred_element_type=f32)
    )
    r.message[...] = pack(image, extra)


def dual_step(k, r):
    n = r.demand.shape[0] // 2
    step_dual = step_scale * r.omega[0:1, :]
    both = (r.own[...].astype(f32) + r.opposite[...].astype(f32)) + (
        r.before[...].astype(f32) + r.after[...].astype(f32)
    )
    r.image[pl.ds(0, n, stride=2), :] = both[0:n, :]
    r.image[pl.ds(1, n, stride=2), :] = both[n : 2 * n, :]
    y = r.y[...]
    y_next = jnp.maximum(y + step_dual * (r.demand[...] - r.image[...]), 0.0)
    if k == ITERS - 1:
        r.y_out[...] = y_next
        return
    tail = both[2 * n :, :]
    r.drift_out[...] = jnp.broadcast_to(tail[0:1, :] + tail[1:2, :] + tail[2:3, :], (8, HALF))
    extra = average(r, k, y_next, y, r.y_out, 1)
    products(r.ints, AT_ROWS, r.y_out, r.blocks, r.found)
    to_peers(r, extra)


def shards(
    block_values,
    block_rows,
    block_cols,
    live_count,
    objective,
    upper_bound,
    demand,
    primal_start,
    dual_start,
    restart_at,
):
    blocks = block_values[0, 0]
    rows = block_rows[0, 0]
    cols = block_cols[0, 0]
    slots, size = blocks.shape[0], blocks.shape[1]
    peers = lax.axis_size(XY)
    depth = lax.axis_size("col")
    total_cols = objective.shape[0] * depth
    total_rows = demand.shape[0] * lax.axis_size(ROW)
    stored = {
        name: vector.reshape(-1, HALF)
        for name, vector in zip(
            VECTORS, (dual_start, demand, objective, upper_bound, primal_start), strict=True
        )
    }
    n_rows, n_cols = demand.shape[0] // size, objective.shape[0] // size
    big, small, one = ((2 * n_cols, HALF), f32), ((2 * n_rows, HALF), f32), ((8, HALF), f32)
    to_all = ((peers, 2 * slots + 16, HALF), bf16)
    to_column = ((2 * n_rows + 16, HALF), bf16)
    half = ((2 * n_cols + 8, HALF), f32)
    chosen = ((n_cols, peers * slots), bf16)
    found = pltpu.VMEM((slots, size), f32)
    work = 2 * slots * size * size * 8
    fill = functools.partial(jnp.zeros, dtype=jnp.int32)
    ints = jnp.concatenate([cols, rows, live_count[0], fill(7), restart_at, fill(112)])
    index = ints.reshape(2, HALF)
    ints = {"ints": ints}
    made = call(
        first_dual,
        "first_dual",
        ints,
        {"index": index, "stored": blocks} | {v + "_stored": a for v, a in stored.items()},
        {
            "blocks": ((2 * slots, size, size), bf16),
            "message": to_all,
            "picked": ((n_rows, slots), bf16),
        }
        | {v: (a.shape, f32) for v, a in stored.items()},
        {
            "found": found,
            "arrivals": pltpu.SemaphoreType.DMA((slots // CHUNK,)),
            "vector_arrivals": pltpu.SemaphoreType.DMA((len(VECTORS),)),
        },
        ("stored", *(v + "_stored" for v in VECTORS)),
        ("blocks", *VECTORS),
        work,
    )
    blocks, message, picked = made["blocks"], made["message"], made["picked"]
    y, want, cost, bound, x = (made[v] for v in VECTORS)
    state_x, state_y, omega, drift, told = {}, {}, {}, {}, {}
    for k in range(ITERS):
        arrived = lax.all_to_all(message, XY, 0, 0, tiled=True)
        made = call(
            functools.partial(sum_columns, k),
            f"sum_columns_{k}",
            {},
            {"arrived": arrived} | told,
            {"half": half} | ({"told": chosen} if k == 0 else {}),
            {"lined": pltpu.VMEM((peers * slots, size), bf16)},
        )
        here = made["half"]
        if k == 0:
            told = {"chosen": made["told"]}
        there = lax.ppermute(here, CORE, [(0, 1), (1, 0)])
        averaged = k < LAST_RESTART
        sums = ("sum_out", "anchor_out") if averaged else ()
        if k > LAST_RESTART:
            state_x, state_y = {}, {}
        made = call(
            functools.partial(primal_step, k, total_cols, total_rows),
            f"primal_step_{k}",
            ints,
            {"here": here, "there": there, "cost": cost, "bound": bound, "x": x}
            | state_x
            | omega
            | drift
            | {"picked": picked, "blocks": blocks},
            {"x_out": big, "omega_out": one, "message": to_column} | dict.fromkeys(sums, big),
            {"extrap": pltpu.VMEM(*big), "found": found},
            held=("blocks",),
            flops=work,
        )
        x, part, omega = made["x_out"], made["message"], {"omega": made["omega_out"]}
        if averaged:
            state_x = {"sum": made["sum_out"], "anchor": made["anchor_out"]}
        after, before, opposite = (
            lax.ppermute(part, "col", [(i, (i + d) % depth) for i in range(depth)])
            for d in (1, 3, 2)
        )
        parts = {"own": part, "before": before, "opposite": opposite, "after": after}
        image = {"image": pltpu.VMEM(*small)}
        if k == ITERS - 1:
            made = call(
                functools.partial(dual_step, k),
                f"dual_step_{k}",
                {},
                parts | {"demand": want, "y": y} | omega,
                {"y_out": small},
                image,
            )
            y = made["y_out"]
        else:
            made = call(
                functools.partial(dual_step, k),
                f"dual_step_{k}",
                ints,
                parts | {"demand": want, "y": y} | omega | state_y | {"blocks": blocks},
                {"y_out": small, "drift_out": one, "message": to_all} | dict.fromkeys(sums, small),
                image | {"found": found},
                held=("blocks",),
                flops=work,
            )
            y, message, drift = made["y_out"], made["message"], {"drift": made["drift_out"]}
            if averaged:
                state_y = {"sum": made["sum_out"], "anchor": made["anchor_out"]}
    return (x.reshape(-1), y.reshape(-1))


def solution(mesh):
    torus = Mesh(
        mesh.devices.reshape(4, 4, 2, mesh.shape["col"]), ("row_0", "row_1", "row_2", "col")
    )
    return jax.shard_map(
        shards,
        mesh=torus,
        in_specs=(
            P(ROW, "col", None, None, None),
            P(ROW, "col", None),
            P(ROW, "col", None),
            P(ROW, "col"),
            P("col"),
            P("col"),
            P(ROW),
            P("col"),
            P(ROW),
            P(),
        ),
        out_specs=(P("col"), P(ROW)),
        check_vma=False,
    )
```

```python
import functools
import types

import jax
import jax.numpy as jnp
from jax import lax
from jax.experimental import pallas as pl
from jax.experimental.pallas import tpu as pltpu
from jax.sharding import Mesh
from jax.sharding import PartitionSpec as P

ITERS = 8
XY = ("row_0", "row_1")
CORE = "row_2"
ROW = ("row_0", "row_1", "row_2")
HALF = 128
CHUNK = 8
UNROLL = 64
LAST_RESTART = ITERS - 3
AT_COLS, AT_ROWS, AT_LIVE, AT_RESTART = 0, 64, 128, 136

step_scale = 0.3
epsilon = 1e-06

f32, bf16 = jnp.float32, jnp.bfloat16
VECTORS = ("y", "demand", "cost", "bound", "x")


def call(body, name, scalars, arrays, outs, scratch, outside=(), held=(), flops=0):
    names = [*scalars, *arrays, *outs, *scratch]

    def run(*refs):
        body(types.SimpleNamespace(**dict(zip(names, refs, strict=True))))

    def spec(key):
        return pl.BlockSpec(memory_space=pltpu.HBM if key in outside else pltpu.VMEM)

    def placed(key, array):
        space = pltpu.HBM if key in outside else pltpu.VMEM
        return pltpu.with_memory_space_constraint(array, space) if key in (*outside, *held) else array

    results = pl.pallas_call(
        run,
        name=name,
        in_specs=[pl.BlockSpec(memory_space=pltpu.SMEM)] * len(scalars) + [spec(k) for k in arrays],
        out_specs=[spec(k) for k in outs],
        out_shape=[
            pltpu.VMEM(*o) if k in held else jax.ShapeDtypeStruct(*o) for k, o in outs.items()
        ],
        scratch_shapes=list(scratch.values()),
        compiler_params=pltpu.CompilerParams(vmem_limit_bytes=24 << 20),
        cost_estimate=pl.CostEstimate(flops=flops, bytes_accessed=flops // 8, transcendentals=0),
    )(*scalars.values(), *(placed(k, a) for k, a in arrays.items()))
    return dict(zip(outs, results, strict=True))


def split_halves(ref, values):
    n = values.shape[0]
    ref[pl.ds(0, n, stride=2), :] = values[:, :HALF]
    ref[pl.ds(1, n, stride=2), :] = values[:, HALF:]


def products(index, offset, source, blocks, target, base=0, first=0, count=None):
    def step(t, carry):
        at = 2 * index[offset + t]
        piece = jnp.concatenate([source[pl.ds(at, 1), :], source[pl.ds(at + 1, 1), :]], axis=1)
        target[pl.ds(t, 1), :] = jnp.dot(
            piece.astype(bf16), blocks[base + t], preferred_element_type=f32
        )
        return carry

    count = target.shape[0] if count is None else count
    lax.fori_loop(first, first + count, step, 0, unroll=min(count, UNROLL))


def in_rows(total, first):
    row = lax.broadcasted_iota(jnp.int32, (16, HALF), 0)
    whole = jnp.full((16, HALF), total, f32)
    high = whole.astype(bf16).astype(f32)
    middle = (whole - high).astype(bf16).astype(f32)
    low = whole - high - middle
    zero = jnp.zeros_like(whole)
    return jnp.where(
        row == first,
        high,
        jnp.where(row == first + 1, middle, jnp.where(row == first + 2, low, zero)),
    )


def restarts(r, j):
    return r.ints[AT_RESTART + j] == 1


def taken_by(r, k):
    taken = jnp.int32(1)
    for j in range(k):
        taken = jnp.where(restarts(r, j), 1, taken + 1)
    return taken.astype(f32)


def pack(values, extra):
    parts = [values[:, :HALF], values[:, HALF:]] + ([] if extra is None else [extra])
    return jnp.concatenate([p.astype(bf16) for p in parts], axis=0)


def to_peers(r, extra):
    slot = lax.broadcasted_iota(jnp.int32, r.found.shape, 0)
    packed = pack(jnp.where(slot < r.ints[AT_LIVE], r.found[...], 0.0), extra)
    for p in range(r.message.shape[0]):
        r.message[p] = packed


def average(r, k, new, old, now, row):
    if k > LAST_RESTART:
        now[...] = new
        return None
    is_restart = restarts(r, k)
    summed, anchor = (new, old) if k == 0 else (r.sum[...] + new, r.anchor[...])
    mean = summed / taken_by(r, k)
    gap = mean - anchor
    now[...] = jnp.where(is_restart, mean, new)
    if k < LAST_RESTART:
        r.anchor_out[...] = jnp.where(is_restart, mean, anchor)
        r.sum_out[...] = jnp.where(is_restart, 0.0, summed)
    return in_rows(jnp.sum(gap * gap), row)


def first_dual(r):
    slots = r.stored.shape[0]
    vectors = [
        pltpu.make_async_copy(getattr(r, v + "_stored"), getattr(r, v), r.vector_arrivals.at[i])
        for i, v in enumerate(VECTORS)
    ]
    copies = [
        pltpu.make_async_copy(
            r.stored.at[pl.ds(c * CHUNK, CHUNK)],
            r.blocks.at[pl.ds(c * CHUNK, CHUNK)],
            r.arrivals.at[c],
        )
        for c in range(slots // CHUNK)
    ]
    for copy in (vectors[0], *copies, *vectors[1:]):
        copy.start()
    cols_then_rows = jnp.broadcast_to(r.index[0:1, :], (16, HALF))
    here = pltpu.roll(cols_then_rows, HALF - slots, 1)[0:1, :slots]
    here = jnp.broadcast_to(here, r.picked.shape)
    row = lax.broadcasted_iota(jnp.int32, r.picked.shape, 0)
    slot = lax.broadcasted_iota(jnp.int32, r.picked.shape, 1)
    r.picked[...] = jnp.where((here == row) & (slot < r.ints[AT_LIVE]), 1.0, 0.0).astype(bf16)
    vectors[0].wait()
    for c, copy in enumerate(copies):
        copy.wait()
        products(r.ints, AT_ROWS, r.y, r.blocks, r.found, 0, c * CHUNK, CHUNK)
        for t in range(c * CHUNK, (c + 1) * CHUNK):
            r.blocks[slots + t] = r.blocks[t].T
    row = lax.broadcasted_iota(jnp.int32, (16, HALF), 0)
    to_peers(r, jnp.where(row == 0, cols_then_rows.astype(f32), 0.0))
    for copy in vectors[1:]:
        copy.wait()


def sum_columns(k, r):
    peers = r.arrived.shape[0]
    slots = r.lined.shape[0] // peers
    chosen = r.told if k == 0 else r.chosen
    has_tail = r.arrived.shape[1] > 2 * slots
    tail = jnp.zeros((16, HALF), f32)
    for p in range(peers):
        r.lined[p * slots : (p + 1) * slots, :HALF] = r.arrived[p, :slots, :]
        r.lined[p * slots : (p + 1) * slots, HALF:] = r.arrived[p, slots : 2 * slots, :]
        if has_tail:
            tail = tail + r.arrived[p, 2 * slots :, :].astype(f32)
    if k == 0:
        shape = (chosen.shape[0], HALF)
        block = lax.broadcasted_iota(jnp.int32, shape, 0).astype(f32)
        early = lax.broadcasted_iota(jnp.int32, (1, HALF), 1) < slots
        for p in range(0, peers, 2):
            pair = [r.arrived[q, 2 * slots :, :].astype(f32) for q in (p, p + 1)]
            told = jnp.where(early, pair[0][0:1, :], pltpu.roll(pair[1], slots, 1)[0:1, :])
            told = jnp.broadcast_to(told, shape)
            chosen[:, p * slots : (p + 2) * slots] = jnp.where(told == block, 1.0, 0.0).astype(bf16)
    n = chosen.shape[0]
    split_halves(r.half, jnp.dot(chosen[...], r.lined[...], preferred_element_type=f32))
    if has_tail:
        total = tail[1:2, :] + tail[2:3, :] + tail[3:4, :]
        r.half[2 * n : 2 * n + 8, :] = jnp.broadcast_to(total, (8, HALF))


def primal_step(k, total_cols, total_rows, r):
    n = r.cost.shape[0]
    omega = jnp.ones((1, HALF), f32) if k == 0 else r.omega[0:1, :]
    if 1 <= k <= LAST_RESTART + 1:
        drift_x = r.drift[0:1, :] / total_cols + epsilon
        drift_y = (r.here[n : n + 1, :] + r.there[n : n + 1, :]) / total_rows + epsilon
        later = jnp.sqrt(omega) * jnp.sqrt(jnp.sqrt(drift_x / drift_y))
        omega = jnp.where(restarts(r, k - 1), later, omega)
    r.omega_out[...] = jnp.broadcast_to(omega, r.omega_out.shape)
    step_primal = step_scale / omega
    dual_image = r.here[0:n, :] + r.there[0:n, :]
    x = r.x[...]
    x_next = jnp.minimum(
        jnp.maximum(x - step_primal * (r.cost[...] - dual_image), 0.0), r.bound[...]
    )
    r.extrap[...] = 2.0 * x_next - x
    extra = average(r, k, x_next, x, r.x_out, 0)
    products(r.ints, AT_COLS, r.extrap, r.blocks, r.found, r.found.shape[0])
    values = r.found[...]
    high = values.astype(bf16)
    rest = values - high.astype(f32)
    middle = rest.astype(bf16)
    low = (rest - middle.astype(f32)).astype(bf16)
    picked = r.picked[...]
    image = (
        jnp.dot(picked, low, preferred_element_type=f32)
        + jnp.dot(picked, middle, preferred_element_type=f32)
        + jnp.dot(picked, high, preferred_element_type=f32)
    )
    r.message[...] = pack(image, extra)


def dual_step(k, r):
    n = r.demand.shape[0] // 2
    step_dual = step_scale * r.omega[0:1, :]
    both = (r.own[...].astype(f32) + r.opposite[...].astype(f32)) + (
        r.before[...].astype(f32) + r.after[...].astype(f32)
    )
    r.image[pl.ds(0, n, stride=2), :] = both[0:n, :]
    r.image[pl.ds(1, n, stride=2), :] = both[n : 2 * n, :]
    y = r.y[...]
    y_next = jnp.maximum(y + step_dual * (r.demand[...] - r.image[...]), 0.0)
    if k == ITERS - 1:
        r.y_out[...] = y_next
        return
    if k <= LAST_RESTART:
        tail = both[2 * n :, :]
        r.drift_out[...] = jnp.broadcast_to(tail[0:1, :] + tail[1:2, :] + tail[2:3, :], (8, HALF))
    extra = average(r, k, y_next, y, r.y_out, 1)
    products(r.ints, AT_ROWS, r.y_out, r.blocks, r.found)
    to_peers(r, extra)


def shards(
    block_values,
    block_rows,
    block_cols,
    live_count,
    objective,
    upper_bound,
    demand,
    primal_start,
    dual_start,
    restart_at,
):
    blocks = block_values[0, 0]
    rows = block_rows[0, 0]
    cols = block_cols[0, 0]
    slots, size = blocks.shape[0], blocks.shape[1]
    peers = lax.axis_size(XY)
    depth = lax.axis_size("col")
    total_cols = objective.shape[0] * depth
    total_rows = demand.shape[0] * lax.axis_size(ROW)
    stored = {
        name: vector.reshape(-1, HALF)
        for name, vector in zip(
            VECTORS, (dual_start, demand, objective, upper_bound, primal_start), strict=True
        )
    }
    n_rows, n_cols = demand.shape[0] // size, objective.shape[0] // size
    big, small, one = ((2 * n_cols, HALF), f32), ((2 * n_rows, HALF), f32), ((8, HALF), f32)

    def to_all(k):
        return ((peers, 2 * slots + 16 * (k <= LAST_RESTART), HALF), bf16)

    def to_column(k):
        return ((2 * n_rows + 16 * (k <= LAST_RESTART), HALF), bf16)

    chosen = ((n_cols, peers * slots), bf16)
    found = pltpu.VMEM((slots, size), f32)
    work = 2 * slots * size * size * 8
    fill = functools.partial(jnp.zeros, dtype=jnp.int32)
    ints = jnp.concatenate([cols, rows, live_count[0], fill(7), restart_at, fill(112)])
    index = ints.reshape(2, HALF)
    ints = {"ints": ints}
    made = call(
        first_dual,
        "first_dual",
        ints,
        {"index": index, "stored": blocks} | {v + "_stored": a for v, a in stored.items()},
        {
            "blocks": ((2 * slots, size, size), bf16),
            "message": to_all(0),
            "picked": ((n_rows, slots), bf16),
        }
        | {v: (a.shape, f32) for v, a in stored.items()},
        {
            "found": found,
            "arrivals": pltpu.SemaphoreType.DMA((slots // CHUNK,)),
            "vector_arrivals": pltpu.SemaphoreType.DMA((len(VECTORS),)),
        },
        ("stored", *(v + "_stored" for v in VECTORS)),
        ("blocks", *VECTORS),
        work,
    )
    blocks, message, picked = made["blocks"], made["message"], made["picked"]
    y, want, cost, bound, x = (made[v] for v in VECTORS)
    state_x, state_y, omega, drift, told = {}, {}, {}, {}, {}
    for k in range(ITERS):
        arrived = lax.all_to_all(message, XY, 0, 0, tiled=True)
        made = call(
            functools.partial(sum_columns, k),
            f"sum_columns_{k}",
            {},
            {"arrived": arrived} | told,
            {"half": ((2 * n_cols + 8 * (k <= LAST_RESTART + 1), HALF), f32)}
            | ({"told": chosen} if k == 0 else {}),
            {"lined": pltpu.VMEM((peers * slots, size), bf16)},
        )
        here = made["half"]
        if k == 0:
            told = {"chosen": made["told"]}
        there = lax.ppermute(here, CORE, [(0, 1), (1, 0)])
        averaged = k < LAST_RESTART
        sums = ("sum_out", "anchor_out") if averaged else ()
        if k > LAST_RESTART:
            state_x, state_y = {}, {}
        made = call(
            functools.partial(primal_step, k, total_cols, total_rows),
            f"primal_step_{k}",
            ints,
            {"here": here, "there": there, "cost": cost, "bound": bound, "x": x}
            | state_x
            | omega
            | drift
            | {"picked": picked, "blocks": blocks},
            {"x_out": big, "omega_out": one, "message": to_column(k)} | dict.fromkeys(sums, big),
            {"extrap": pltpu.VMEM(*big), "found": found},
            held=("blocks",),
            flops=work,
        )
        x, part, omega = made["x_out"], made["message"], {"omega": made["omega_out"]}
        if averaged:
            state_x = {"sum": made["sum_out"], "anchor": made["anchor_out"]}
        after, before, opposite = (
            lax.ppermute(part, "col", [(i, (i + d) % depth) for i in range(depth)])
            for d in (1, 3, 2)
        )
        parts = {"own": part, "after": after, "before": before, "opposite": opposite}
        image = {"image": pltpu.VMEM(*small)}
        if k == ITERS - 1:
            made = call(
                functools.partial(dual_step, k),
                f"dual_step_{k}",
                {},
                parts | {"demand": want, "y": y} | omega,
                {"y_out": small},
                image,
            )
            y = made["y_out"]
        else:
            made = call(
                functools.partial(dual_step, k),
                f"dual_step_{k}",
                ints,
                parts | {"demand": want, "y": y} | omega | state_y | {"blocks": blocks},
                {"y_out": small, "message": to_all(k)}
                | ({"drift_out": one} if k <= LAST_RESTART else {})
                | dict.fromkeys(sums, small),
                image | {"found": found},
                held=("blocks",),
                flops=work,
            )
            y, message = made["y_out"], made["message"]
            drift = {"drift": made["drift_out"]} if k <= LAST_RESTART else {}
            if averaged:
                state_y = {"sum": made["sum_out"], "anchor": made["anchor_out"]}
    return (x.reshape(-1), y.reshape(-1))


def solution(mesh):
    torus = Mesh(
        mesh.devices.reshape(4, 4, 2, mesh.shape["col"]), ("row_0", "row_1", "row_2", "col")
    )
    return jax.shard_map(
        shards,
        mesh=torus,
        in_specs=(
            P(ROW, "col", None, None, None),
            P(ROW, "col", None),
            P(ROW, "col", None),
            P(ROW, "col"),
            P("col"),
            P("col"),
            P(ROW),
            P("col"),
            P(ROW),
            P(),
        ),
        out_specs=(P("col"), P(ROW)),
        check_vma=False,
    )
```

```python
import functools
import types

import jax
import jax.numpy as jnp
from jax import lax
from jax.experimental import pallas as pl
from jax.experimental.pallas import tpu as pltpu
from jax.sharding import Mesh
from jax.sharding import PartitionSpec as P

ITERS = 8
XY = ("row_0", "row_1")
CORE = "row_2"
ROW = ("row_0", "row_1", "row_2")
HALF = 128
CHUNK = 8
UNROLL = 64
LAST_RESTART = ITERS - 3
AT_COLS, AT_ROWS, AT_LIVE, AT_RESTART = 0, 64, 128, 136

step_scale = 0.3
epsilon = 1e-06

f32, bf16 = jnp.float32, jnp.bfloat16
VECTORS = ("demand", "cost", "bound", "x")


def call(body, name, scalars, arrays, outs, scratch, outside=(), held=(), flops=0):
    names = [*scalars, *arrays, *outs, *scratch]

    def run(*refs):
        body(types.SimpleNamespace(**dict(zip(names, refs, strict=True))))

    def spec(key):
        return pl.BlockSpec(memory_space=pltpu.HBM if key in outside else pltpu.VMEM)

    def placed(key, array):
        space = pltpu.HBM if key in outside else pltpu.VMEM
        return pltpu.with_memory_space_constraint(array, space) if key in (*outside, *held) else array

    results = pl.pallas_call(
        run,
        name=name,
        in_specs=[pl.BlockSpec(memory_space=pltpu.SMEM)] * len(scalars) + [spec(k) for k in arrays],
        out_specs=[spec(k) for k in outs],
        out_shape=[
            pltpu.VMEM(*o) if k in held else jax.ShapeDtypeStruct(*o) for k, o in outs.items()
        ],
        scratch_shapes=list(scratch.values()),
        compiler_params=pltpu.CompilerParams(vmem_limit_bytes=24 << 20),
        cost_estimate=pl.CostEstimate(flops=flops, bytes_accessed=flops // 8, transcendentals=0),
    )(*scalars.values(), *(placed(k, a) for k, a in arrays.items()))
    return dict(zip(outs, results, strict=True))


def split_halves(ref, values):
    n = values.shape[0]
    ref[pl.ds(0, n, stride=2), :] = values[:, :HALF]
    ref[pl.ds(1, n, stride=2), :] = values[:, HALF:]


def products(index, offset, source, blocks, target, base=0, first=0, count=None):
    def step(t, carry):
        at = 2 * index[offset + t]
        piece = jnp.concatenate([source[pl.ds(at, 1), :], source[pl.ds(at + 1, 1), :]], axis=1)
        target[pl.ds(t, 1), :] = jnp.dot(
            piece.astype(bf16), blocks[base + t], preferred_element_type=f32
        )
        return carry

    count = target.shape[0] if count is None else count
    lax.fori_loop(first, first + count, step, 0, unroll=min(count, UNROLL))


def in_rows(total, first):
    row = lax.broadcasted_iota(jnp.int32, (16, HALF), 0)
    whole = jnp.full((16, HALF), total, f32)
    high = whole.astype(bf16).astype(f32)
    middle = (whole - high).astype(bf16).astype(f32)
    low = whole - high - middle
    zero = jnp.zeros_like(whole)
    return jnp.where(
        row == first,
        high,
        jnp.where(row == first + 1, middle, jnp.where(row == first + 2, low, zero)),
    )


def restarts(r, j):
    return r.ints[AT_RESTART + j] == 1


def taken_by(r, k):
    taken = jnp.int32(1)
    for j in range(k):
        taken = jnp.where(restarts(r, j), 1, taken + 1)
    return taken.astype(f32)


def pack(values, extra):
    parts = [values[:, :HALF], values[:, HALF:]] + ([] if extra is None else [extra])
    return jnp.concatenate([p.astype(bf16) for p in parts], axis=0)


def to_peers(r, extra):
    slot = lax.broadcasted_iota(jnp.int32, r.found.shape, 0)
    packed = pack(jnp.where(slot < r.ints[AT_LIVE], r.found[...], 0.0), extra)
    for p in range(r.message.shape[0]):
        r.message[p] = packed


def average(r, k, new, old, now, row):
    if k > LAST_RESTART:
        now[...] = new
        return None
    is_restart = restarts(r, k)
    summed, anchor = (new, old) if k == 0 else (r.sum[...] + new, r.anchor[...])
    mean = summed / taken_by(r, k)
    gap = mean - anchor
    now[...] = jnp.where(is_restart, mean, new)
    if k < LAST_RESTART:
        r.anchor_out[...] = jnp.where(is_restart, mean, anchor)
        r.sum_out[...] = jnp.where(is_restart, 0.0, summed)
    return in_rows(jnp.sum(gap * gap), row)


def first_dual(r):
    slots = r.stored.shape[0]
    first = pltpu.make_async_copy(r.y_stored, r.y, r.y_arrival)
    copies = [
        pltpu.make_async_copy(
            r.stored.at[pl.ds(c * CHUNK, CHUNK)],
            r.blocks.at[pl.ds(c * CHUNK, CHUNK)],
            r.arrivals.at[c],
        )
        for c in range(slots // CHUNK)
    ]
    for copy in (first, *copies):
        copy.start()
    cols_then_rows = jnp.broadcast_to(r.index[0:1, :], (16, HALF))
    here = pltpu.roll(cols_then_rows, HALF - slots, 1)[0:1, :slots]
    here = jnp.broadcast_to(here, r.picked.shape)
    row = lax.broadcasted_iota(jnp.int32, r.picked.shape, 0)
    slot = lax.broadcasted_iota(jnp.int32, r.picked.shape, 1)
    r.picked[...] = jnp.where((here == row) & (slot < r.ints[AT_LIVE]), 1.0, 0.0).astype(bf16)
    first.wait()
    for c, copy in enumerate(copies):
        copy.wait()
        products(r.ints, AT_ROWS, r.y, r.blocks, r.found, 0, c * CHUNK, CHUNK)
        for t in range(c * CHUNK, (c + 1) * CHUNK):
            r.blocks[slots + t] = r.blocks[t].T
    row = lax.broadcasted_iota(jnp.int32, (16, HALF), 0)
    to_peers(r, jnp.where(row == 0, cols_then_rows.astype(f32), 0.0))


def bring(names, r):
    copies = [
        pltpu.make_async_copy(getattr(r, v + "_stored"), getattr(r, v), r.arrivals.at[i])
        for i, v in enumerate(names)
    ]
    for copy in copies:
        copy.start()
    for copy in copies:
        copy.wait()


def sum_columns(k, r):
    peers = r.arrived.shape[0]
    slots = r.lined.shape[0] // peers
    chosen = r.told if k == 0 else r.chosen
    has_tail = r.arrived.shape[1] > 2 * slots
    tail = jnp.zeros((16, HALF), f32)
    for p in range(peers):
        r.lined[p * slots : (p + 1) * slots, :HALF] = r.arrived[p, :slots, :]
        r.lined[p * slots : (p + 1) * slots, HALF:] = r.arrived[p, slots : 2 * slots, :]
        if has_tail:
            tail = tail + r.arrived[p, 2 * slots :, :].astype(f32)
    if k == 0:
        shape = (chosen.shape[0], HALF)
        block = lax.broadcasted_iota(jnp.int32, shape, 0).astype(f32)
        early = lax.broadcasted_iota(jnp.int32, (1, HALF), 1) < slots
        for p in range(0, peers, 2):
            pair = [r.arrived[q, 2 * slots :, :].astype(f32) for q in (p, p + 1)]
            told = jnp.where(early, pair[0][0:1, :], pltpu.roll(pair[1], slots, 1)[0:1, :])
            told = jnp.broadcast_to(told, shape)
            chosen[:, p * slots : (p + 2) * slots] = jnp.where(told == block, 1.0, 0.0).astype(bf16)
    n = chosen.shape[0]
    split_halves(r.half, jnp.dot(chosen[...], r.lined[...], preferred_element_type=f32))
    if has_tail:
        total = tail[1:2, :] + tail[2:3, :] + tail[3:4, :]
        r.half[2 * n : 2 * n + 8, :] = jnp.broadcast_to(total, (8, HALF))


def primal_step(k, total_cols, total_rows, r):
    n = r.cost.shape[0]
    omega = jnp.ones((1, HALF), f32) if k == 0 else r.omega[0:1, :]
    if 1 <= k <= LAST_RESTART + 1:
        drift_x = r.drift[0:1, :] / total_cols + epsilon
        drift_y = (r.here[n : n + 1, :] + r.there[n : n + 1, :]) / total_rows + epsilon
        later = jnp.sqrt(omega) * jnp.sqrt(jnp.sqrt(drift_x / drift_y))
        omega = jnp.where(restarts(r, k - 1), later, omega)
    r.omega_out[...] = jnp.broadcast_to(omega, r.omega_out.shape)
    step_primal = step_scale / omega
    dual_image = r.here[0:n, :] + r.there[0:n, :]
    x = r.x[...]
    x_next = jnp.minimum(
        jnp.maximum(x - step_primal * (r.cost[...] - dual_image), 0.0), r.bound[...]
    )
    r.extrap[...] = 2.0 * x_next - x
    extra = average(r, k, x_next, x, r.x_out, 0)
    products(r.ints, AT_COLS, r.extrap, r.blocks, r.found, r.found.shape[0])
    values = r.found[...]
    high = values.astype(bf16)
    low = (values - high.astype(f32)).astype(bf16)
    picked = r.picked[...]
    image = jnp.dot(picked, low, preferred_element_type=f32) + jnp.dot(
        picked, high, preferred_element_type=f32
    )
    r.message[...] = pack(image, extra)


def dual_step(k, r):
    n = r.demand.shape[0] // 2
    step_dual = step_scale * r.omega[0:1, :]
    both = (r.own[...].astype(f32) + r.opposite[...].astype(f32)) + (
        r.before[...].astype(f32) + r.after[...].astype(f32)
    )
    r.image[pl.ds(0, n, stride=2), :] = both[0:n, :]
    r.image[pl.ds(1, n, stride=2), :] = both[n : 2 * n, :]
    y = r.y[...]
    y_next = jnp.maximum(y + step_dual * (r.demand[...] - r.image[...]), 0.0)
    if k == ITERS - 1:
        r.y_out[...] = y_next
        return
    if k <= LAST_RESTART:
        tail = both[2 * n :, :]
        r.drift_out[...] = jnp.broadcast_to(tail[0:1, :] + tail[1:2, :] + tail[2:3, :], (8, HALF))
    extra = average(r, k, y_next, y, r.y_out, 1)
    products(r.ints, AT_ROWS, r.y_out, r.blocks, r.found)
    to_peers(r, extra)


def shards(
    block_values,
    block_rows,
    block_cols,
    live_count,
    objective,
    upper_bound,
    demand,
    primal_start,
    dual_start,
    restart_at,
):
    blocks = block_values[0, 0]
    rows = block_rows[0, 0]
    cols = block_cols[0, 0]
    slots, size = blocks.shape[0], blocks.shape[1]
    peers = lax.axis_size(XY)
    depth = lax.axis_size("col")
    total_cols = objective.shape[0] * depth
    total_rows = demand.shape[0] * lax.axis_size(ROW)
    stored = {
        name: vector.reshape(-1, HALF)
        for name, vector in zip(
            VECTORS, (demand, objective, upper_bound, primal_start), strict=True
        )
    }
    n_rows, n_cols = demand.shape[0] // size, objective.shape[0] // size
    big, small, one = ((2 * n_cols, HALF), f32), ((2 * n_rows, HALF), f32), ((8, HALF), f32)

    def to_all(k):
        return ((peers, 2 * slots + 16 * (k <= LAST_RESTART), HALF), bf16)

    def to_column(k):
        return ((2 * n_rows + 16 * (k <= LAST_RESTART), HALF), bf16)

    chosen = ((n_cols, peers * slots), bf16)
    found = pltpu.VMEM((slots, size), f32)
    work = 2 * slots * size * size * 8
    fill = functools.partial(jnp.zeros, dtype=jnp.int32)
    ints = jnp.concatenate([cols, rows, live_count[0], fill(7), restart_at, fill(112)])
    index = ints.reshape(2, HALF)
    ints = {"ints": ints}
    made = call(
        first_dual,
        "first_dual",
        ints,
        {"index": index, "stored": blocks, "y_stored": dual_start.reshape(-1, HALF)},
        {
            "blocks": ((2 * slots, size, size), bf16),
            "message": to_all(0),
            "picked": ((n_rows, slots), bf16),
            "y": small,
        },
        {
            "found": found,
            "arrivals": pltpu.SemaphoreType.DMA((slots // CHUNK,)),
            "y_arrival": pltpu.SemaphoreType.DMA,
        },
        ("stored", "y_stored"),
        ("blocks", "y"),
        work,
    )
    blocks, message, picked = made["blocks"], made["message"], made["picked"]
    y = made["y"]
    state_x, state_y, omega, drift, told = {}, {}, {}, {}, {}
    for k in range(ITERS):
        arrived = lax.all_to_all(message, XY, 0, 0, tiled=True)
        made = call(
            functools.partial(sum_columns, k),
            f"sum_columns_{k}",
            {},
            {"arrived": arrived} | told,
            {"half": ((2 * n_cols + 8 * (k <= LAST_RESTART + 1), HALF), f32)}
            | ({"told": chosen} if k == 0 else {}),
            {"lined": pltpu.VMEM((peers * slots, size), bf16)},
        )
        here = made["half"]
        if k == 0:
            told = {"chosen": made["told"]}
        there = lax.ppermute(here, CORE, [(0, 1), (1, 0)])
        if k == 0:
            unused, *vectors = lax.optimization_barrier((here, *stored.values()))
            made = call(
                functools.partial(bring, VECTORS),
                "bring",
                {},
                {v + "_stored": a for v, a in zip(VECTORS, vectors, strict=True)},
                {v: (a.shape, f32) for v, a in stored.items()},
                {"arrivals": pltpu.SemaphoreType.DMA((len(VECTORS),))},
                [v + "_stored" for v in VECTORS],
                VECTORS,
                4 << 20,
            )
            want, cost, bound, x = (made[v] for v in VECTORS)
        averaged = k < LAST_RESTART
        sums = ("sum_out", "anchor_out") if averaged else ()
        if k > LAST_RESTART:
            state_x, state_y = {}, {}
        made = call(
            functools.partial(primal_step, k, total_cols, total_rows),
            f"primal_step_{k}",
            ints,
            {"here": here, "there": there, "cost": cost, "bound": bound, "x": x}
            | state_x
            | omega
            | drift
            | {"picked": picked, "blocks": blocks},
            {"x_out": big, "omega_out": one, "message": to_column(k)} | dict.fromkeys(sums, big),
            {"extrap": pltpu.VMEM(*big), "found": found},
            held=("blocks",) + ("x_out",) * (k == ITERS - 1),
            flops=work,
        )
        x, part, omega = made["x_out"], made["message"], {"omega": made["omega_out"]}
        if averaged:
            state_x = {"sum": made["sum_out"], "anchor": made["anchor_out"]}
        after, before, opposite = (
            lax.ppermute(part, "col", [(i, (i + d) % depth) for i in range(depth)])
            for d in (1, 3, 2)
        )
        parts = {"own": part, "after": after, "before": before, "opposite": opposite}
        image = {"image": pltpu.VMEM(*small)}
        if k == ITERS - 1:
            made = call(
                functools.partial(dual_step, k),
                f"dual_step_{k}",
                {},
                parts | {"demand": want, "y": y} | omega,
                {"y_out": small},
                image,
            )
            y = made["y_out"]
        else:
            made = call(
                functools.partial(dual_step, k),
                f"dual_step_{k}",
                ints,
                parts | {"demand": want, "y": y} | omega | state_y | {"blocks": blocks},
                {"y_out": small, "message": to_all(k)}
                | ({"drift_out": one} if k <= LAST_RESTART else {})
                | dict.fromkeys(sums, small),
                image | {"found": found},
                held=("blocks",),
                flops=work,
            )
            y, message = made["y_out"], made["message"]
            drift = {"drift": made["drift_out"]} if k <= LAST_RESTART else {}
            if averaged:
                state_y = {"sum": made["sum_out"], "anchor": made["anchor_out"]}
    return (x.reshape(-1), y.reshape(-1))


def solution(mesh):
    torus = Mesh(
        mesh.devices.reshape(4, 4, 2, mesh.shape["col"]), ("row_0", "row_1", "row_2", "col")
    )
    return jax.shard_map(
        shards,
        mesh=torus,
        in_specs=(
            P(ROW, "col", None, None, None),
            P(ROW, "col", None),
            P(ROW, "col", None),
            P(ROW, "col"),
            P("col"),
            P("col"),
            P(ROW),
            P("col"),
            P(ROW),
            P(),
        ),
        out_specs=(P("col"), P(ROW)),
        check_vma=False,
    )
```

```python
import functools
import types

import jax
import jax.numpy as jnp
from jax import lax
from jax.experimental import pallas as pl
from jax.experimental.pallas import tpu as pltpu
from jax.sharding import Mesh
from jax.sharding import PartitionSpec as P

ITERS = 8
XY = ("row_0", "row_1")
CORE = "row_2"
ROW = ("row_0", "row_1", "row_2")
HALF = 128
CHUNK = 8
UNROLL = 64
LAST_RESTART = ITERS - 3
AT_COLS, AT_ROWS, AT_LIVE, AT_RESTART = 0, 64, 128, 136

step_scale = 0.3
epsilon = 1e-06

f32, bf16 = jnp.float32, jnp.bfloat16
VECTORS = ("y", "demand", "cost", "bound", "x")


def call(body, name, scalars, arrays, outs, scratch, outside=(), held=(), flops=0):
    names = [*scalars, *arrays, *outs, *scratch]

    def run(*refs):
        body(types.SimpleNamespace(**dict(zip(names, refs, strict=True))))

    def spec(key):
        return pl.BlockSpec(memory_space=pltpu.HBM if key in outside else pltpu.VMEM)

    def placed(key, array):
        space = pltpu.HBM if key in outside else pltpu.VMEM
        return pltpu.with_memory_space_constraint(array, space) if key in (*outside, *held) else array

    results = pl.pallas_call(
        run,
        name=name,
        in_specs=[pl.BlockSpec(memory_space=pltpu.SMEM)] * len(scalars) + [spec(k) for k in arrays],
        out_specs=[spec(k) for k in outs],
        out_shape=[
            pltpu.VMEM(*o) if k in held else jax.ShapeDtypeStruct(*o) for k, o in outs.items()
        ],
        scratch_shapes=list(scratch.values()),
        compiler_params=pltpu.CompilerParams(vmem_limit_bytes=24 << 20),
        cost_estimate=pl.CostEstimate(flops=flops, bytes_accessed=flops // 8, transcendentals=0),
    )(*scalars.values(), *(placed(k, a) for k, a in arrays.items()))
    return dict(zip(outs, results, strict=True))


def split_halves(ref, values):
    n = values.shape[0]
    ref[pl.ds(0, n, stride=2), :] = values[:, :HALF]
    ref[pl.ds(1, n, stride=2), :] = values[:, HALF:]


def products(index, offset, source, blocks, target, base=0, first=0, count=None):
    def step(t, carry):
        at = 2 * index[offset + t]
        piece = jnp.concatenate([source[pl.ds(at, 1), :], source[pl.ds(at + 1, 1), :]], axis=1)
        target[pl.ds(t, 1), :] = jnp.dot(
            piece.astype(bf16), blocks[base + t], preferred_element_type=f32
        )
        return carry

    count = target.shape[0] if count is None else count
    lax.fori_loop(first, first + count, step, 0, unroll=min(count, UNROLL))


def in_rows(total, first):
    row = lax.broadcasted_iota(jnp.int32, (16, HALF), 0)
    whole = jnp.full((16, HALF), total, f32)
    high = whole.astype(bf16).astype(f32)
    middle = (whole - high).astype(bf16).astype(f32)
    low = whole - high - middle
    zero = jnp.zeros_like(whole)
    return jnp.where(
        row == first,
        high,
        jnp.where(row == first + 1, middle, jnp.where(row == first + 2, low, zero)),
    )


def restarts(r, j):
    return r.ints[AT_RESTART + j] == 1


def taken_by(r, k):
    taken = jnp.int32(1)
    for j in range(k):
        taken = jnp.where(restarts(r, j), 1, taken + 1)
    return taken.astype(f32)


def pack(values, extra):
    parts = [values[:, :HALF], values[:, HALF:]] + ([] if extra is None else [extra])
    return jnp.concatenate([p.astype(bf16) for p in parts], axis=0)


def to_peers(r, extra):
    slot = lax.broadcasted_iota(jnp.int32, r.found.shape, 0)
    packed = pack(jnp.where(slot < r.ints[AT_LIVE], r.found[...], 0.0), extra)
    for p in range(r.message.shape[0]):
        r.message[p] = packed


def average(r, k, new, old, now, row):
    if k > LAST_RESTART:
        now[...] = new
        return None
    is_restart = restarts(r, k)
    summed, anchor = (new, old) if k == 0 else (r.sum[...] + new, r.anchor[...])
    mean = summed / taken_by(r, k)
    gap = mean - anchor
    now[...] = jnp.where(is_restart, mean, new)
    if k < LAST_RESTART:
        r.anchor_out[...] = jnp.where(is_restart, mean, anchor)
        r.sum_out[...] = jnp.where(is_restart, 0.0, summed)
    return in_rows(jnp.sum(gap * gap), row)


def first_dual(r):
    slots = r.stored.shape[0]
    vectors = [
        pltpu.make_async_copy(getattr(r, v + "_stored"), getattr(r, v), r.vector_arrivals.at[i])
        for i, v in enumerate(VECTORS)
    ]
    copies = [
        pltpu.make_async_copy(
            r.stored.at[pl.ds(c * CHUNK, CHUNK)],
            r.blocks.at[pl.ds(c * CHUNK, CHUNK)],
            r.arrivals.at[c],
        )
        for c in range(slots // CHUNK)
    ]
    for copy in (vectors[0], *copies, *vectors[1:]):
        copy.start()
    cols_then_rows = jnp.broadcast_to(r.index[0:1, :], (16, HALF))
    here = pltpu.roll(cols_then_rows, HALF - slots, 1)[0:1, :slots]
    here = jnp.broadcast_to(here, r.picked.shape)
    row = lax.broadcasted_iota(jnp.int32, r.picked.shape, 0)
    slot = lax.broadcasted_iota(jnp.int32, r.picked.shape, 1)
    r.picked[...] = jnp.where((here == row) & (slot < r.ints[AT_LIVE]), 1.0, 0.0).astype(bf16)
    vectors[0].wait()
    for c, copy in enumerate(copies):
        copy.wait()
        products(r.ints, AT_ROWS, r.y, r.blocks, r.found, 0, c * CHUNK, CHUNK)
        for t in range(c * CHUNK, (c + 1) * CHUNK):
            r.blocks[slots + t] = r.blocks[t].T
    row = lax.broadcasted_iota(jnp.int32, (16, HALF), 0)
    to_peers(r, jnp.where(row == 0, cols_then_rows.astype(f32), 0.0))
    for copy in vectors[1:]:
        copy.wait()


def sum_columns(k, r):
    peers = r.arrived.shape[0]
    slots = r.lined.shape[0] // peers
    chosen = r.told if k == 0 else r.chosen
    has_tail = r.arrived.shape[1] > 2 * slots
    tail = jnp.zeros((16, HALF), f32)
    for p in range(peers):
        r.lined[p * slots : (p + 1) * slots, :HALF] = r.arrived[p, :slots, :]
        r.lined[p * slots : (p + 1) * slots, HALF:] = r.arrived[p, slots : 2 * slots, :]
        if has_tail:
            tail = tail + r.arrived[p, 2 * slots :, :].astype(f32)
    if k == 0:
        shape = (chosen.shape[0], HALF)
        block = lax.broadcasted_iota(jnp.int32, shape, 0).astype(f32)
        early = lax.broadcasted_iota(jnp.int32, (1, HALF), 1) < slots
        for p in range(0, peers, 2):
            pair = [r.arrived[q, 2 * slots :, :].astype(f32) for q in (p, p + 1)]
            told = jnp.where(early, pair[0][0:1, :], pltpu.roll(pair[1], slots, 1)[0:1, :])
            told = jnp.broadcast_to(told, shape)
            chosen[:, p * slots : (p + 2) * slots] = jnp.where(told == block, 1.0, 0.0).astype(bf16)
    n = chosen.shape[0]
    split_halves(r.half, jnp.dot(chosen[...], r.lined[...], preferred_element_type=f32))
    if has_tail:
        total = tail[1:2, :] + tail[2:3, :] + tail[3:4, :]
        r.half[2 * n : 2 * n + 8, :] = jnp.broadcast_to(total, (8, HALF))


def primal_step(k, total_cols, total_rows, r):
    n = r.cost.shape[0]
    omega = jnp.ones((1, HALF), f32) if k == 0 else r.omega[0:1, :]
    if 1 <= k <= LAST_RESTART + 1:
        drift_x = r.drift[0:1, :] / total_cols + epsilon
        drift_y = (r.here[n : n + 1, :] + r.there[n : n + 1, :]) / total_rows + epsilon
        later = jnp.sqrt(omega) * jnp.sqrt(jnp.sqrt(drift_x / drift_y))
        omega = jnp.where(restarts(r, k - 1), later, omega)
    r.omega_out[...] = jnp.broadcast_to(omega, r.omega_out.shape)
    step_primal = step_scale / omega
    dual_image = r.here[0:n, :] + r.there[0:n, :]
    x = r.x[...]
    x_next = jnp.minimum(
        jnp.maximum(x - step_primal * (r.cost[...] - dual_image), 0.0), r.bound[...]
    )
    r.extrap[...] = 2.0 * x_next - x
    extra = average(r, k, x_next, x, r.x_out, 0)
    products(r.ints, AT_COLS, r.extrap, r.blocks, r.found, r.found.shape[0])
    values = r.found[...]
    high = values.astype(bf16)
    low = (values - high.astype(f32)).astype(bf16)
    picked = r.picked[...]
    image = jnp.dot(picked, low, preferred_element_type=f32) + jnp.dot(
        picked, high, preferred_element_type=f32
    )
    r.message[...] = pack(image, extra)


def dual_step(k, r):
    n = r.demand.shape[0] // 2
    step_dual = step_scale * r.omega[0:1, :]
    both = (r.own[...].astype(f32) + r.opposite[...].astype(f32)) + (
        r.before[...].astype(f32) + r.after[...].astype(f32)
    )
    r.image[pl.ds(0, n, stride=2), :] = both[0:n, :]
    r.image[pl.ds(1, n, stride=2), :] = both[n : 2 * n, :]
    y = r.y[...]
    y_next = jnp.maximum(y + step_dual * (r.demand[...] - r.image[...]), 0.0)
    if k == ITERS - 1:
        r.y_out[...] = y_next
        return
    if k <= LAST_RESTART:
        tail = both[2 * n :, :]
        r.drift_out[...] = jnp.broadcast_to(tail[0:1, :] + tail[1:2, :] + tail[2:3, :], (8, HALF))
    extra = average(r, k, y_next, y, r.y_out, 1)
    products(r.ints, AT_ROWS, r.y_out, r.blocks, r.found)
    to_peers(r, extra)


def shards(
    block_values,
    block_rows,
    block_cols,
    live_count,
    objective,
    upper_bound,
    demand,
    primal_start,
    dual_start,
    restart_at,
):
    blocks = block_values[0, 0]
    rows = block_rows[0, 0]
    cols = block_cols[0, 0]
    slots, size = blocks.shape[0], blocks.shape[1]
    peers = lax.axis_size(XY)
    depth = lax.axis_size("col")
    total_cols = objective.shape[0] * depth
    total_rows = demand.shape[0] * lax.axis_size(ROW)
    stored = {
        name: vector.reshape(-1, HALF)
        for name, vector in zip(
            VECTORS, (dual_start, demand, objective, upper_bound, primal_start), strict=True
        )
    }
    n_rows, n_cols = demand.shape[0] // size, objective.shape[0] // size
    big, small, one = ((2 * n_cols, HALF), f32), ((2 * n_rows, HALF), f32), ((8, HALF), f32)

    def to_all(k):
        return ((peers, 2 * slots + 16 * (k <= LAST_RESTART), HALF), bf16)

    def to_column(k):
        return ((2 * n_rows + 16 * (k <= LAST_RESTART), HALF), bf16)

    chosen = ((n_cols, peers * slots), bf16)
    found = pltpu.VMEM((slots, size), f32)
    work = 2 * slots * size * size * 8
    fill = functools.partial(jnp.zeros, dtype=jnp.int32)
    ints = jnp.concatenate([cols, rows, live_count[0], fill(7), restart_at, fill(112)])
    index = ints.reshape(2, HALF)
    ints = {"ints": ints}
    made = call(
        first_dual,
        "first_dual",
        ints,
        {"index": index, "stored": blocks} | {v + "_stored": a for v, a in stored.items()},
        {
            "blocks": ((2 * slots, size, size), bf16),
            "message": to_all(0),
            "picked": ((n_rows, slots), bf16),
        }
        | {v: (a.shape, f32) for v, a in stored.items()},
        {
            "found": found,
            "arrivals": pltpu.SemaphoreType.DMA((slots // CHUNK,)),
            "vector_arrivals": pltpu.SemaphoreType.DMA((len(VECTORS),)),
        },
        ("stored", *(v + "_stored" for v in VECTORS)),
        ("blocks", *VECTORS),
        work,
    )
    blocks, message, picked = made["blocks"], made["message"], made["picked"]
    y, want, cost, bound, x = (made[v] for v in VECTORS)
    state_x, state_y, omega, drift, told = {}, {}, {}, {}, {}
    for k in range(ITERS):
        arrived = lax.all_to_all(message, XY, 0, 0, tiled=True)
        made = call(
            functools.partial(sum_columns, k),
            f"sum_columns_{k}",
            {},
            {"arrived": arrived} | told,
            {"half": ((2 * n_cols + 8 * (k <= LAST_RESTART + 1), HALF), f32)}
            | ({"told": chosen} if k == 0 else {}),
            {"lined": pltpu.VMEM((peers * slots, size), bf16)},
        )
        here = made["half"]
        if k == 0:
            told = {"chosen": made["told"]}
        there = lax.ppermute(here, CORE, [(0, 1), (1, 0)])
        averaged = k < LAST_RESTART
        sums = ("sum_out", "anchor_out") if averaged else ()
        if k > LAST_RESTART:
            state_x, state_y = {}, {}
        made = call(
            functools.partial(primal_step, k, total_cols, total_rows),
            f"primal_step_{k}",
            ints,
            {"here": here, "there": there, "cost": cost, "bound": bound, "x": x}
            | state_x
            | omega
            | drift
            | {"picked": picked, "blocks": blocks},
            {"x_out": big, "omega_out": one, "message": to_column(k)} | dict.fromkeys(sums, big),
            {"extrap": pltpu.VMEM(*big), "found": found},
            held=("blocks",) + ("x_out",) * (k == ITERS - 1),
            flops=work,
        )
        x, part, omega = made["x_out"], made["message"], {"omega": made["omega_out"]}
        if averaged:
            state_x = {"sum": made["sum_out"], "anchor": made["anchor_out"]}
        after, before, opposite = (
            lax.ppermute(part, "col", [(i, (i + d) % depth) for i in range(depth)])
            for d in (1, 3, 2)
        )
        parts = {"own": part, "after": after, "before": before, "opposite": opposite}
        image = {"image": pltpu.VMEM(*small)}
        if k == ITERS - 1:
            made = call(
                functools.partial(dual_step, k),
                f"dual_step_{k}",
                {},
                parts | {"demand": want, "y": y} | omega,
                {"y_out": small},
                image,
            )
            y = made["y_out"]
        else:
            made = call(
                functools.partial(dual_step, k),
                f"dual_step_{k}",
                ints,
                parts | {"demand": want, "y": y} | omega | state_y | {"blocks": blocks},
                {"y_out": small, "message": to_all(k)}
                | ({"drift_out": one} if k <= LAST_RESTART else {})
                | dict.fromkeys(sums, small),
                image | {"found": found},
                held=("blocks",),
                flops=work,
            )
            y, message = made["y_out"], made["message"]
            drift = {"drift": made["drift_out"]} if k <= LAST_RESTART else {}
            if averaged:
                state_y = {"sum": made["sum_out"], "anchor": made["anchor_out"]}
    return (x.reshape(-1), y.reshape(-1))


def solution(mesh):
    torus = Mesh(
        mesh.devices.reshape(4, 4, 2, mesh.shape["col"]), ("row_0", "row_1", "row_2", "col")
    )
    return jax.shard_map(
        shards,
        mesh=torus,
        in_specs=(
            P(ROW, "col", None, None, None),
            P(ROW, "col", None),
            P(ROW, "col", None),
            P(ROW, "col"),
            P("col"),
            P("col"),
            P(ROW),
            P("col"),
            P(ROW),
            P(),
        ),
        out_specs=(P("col"), P(ROW)),
        check_vma=False,
    )
```

```python
import functools
import types

import jax
import jax.numpy as jnp
from jax import lax
from jax.experimental import pallas as pl
from jax.experimental.pallas import tpu as pltpu
from jax.sharding import Mesh
from jax.sharding import PartitionSpec as P

ITERS = 8
XY = ("row_0", "row_1")
CORE = "row_2"
ROW = ("row_0", "row_1", "row_2")
HALF = 128
CHUNK = 16
UNROLL = 64
LAST_RESTART = ITERS - 3
AT_COLS, AT_ROWS, AT_LIVE, AT_RESTART = 0, 64, 0, 8

step_scale = 0.3
epsilon = 1e-06

f32, bf16 = jnp.float32, jnp.bfloat16
VECTORS = ("y", "demand", "cost", "bound", "x")


def call(body, name, scalars, arrays, outs, scratch, outside=(), held=(), flops=0):
    names = [*scalars, *arrays, *outs, *scratch]

    def run(*refs):
        body(types.SimpleNamespace(**dict(zip(names, refs, strict=True))))

    def spec(key):
        return pl.BlockSpec(memory_space=pltpu.HBM if key in outside else pltpu.VMEM)

    def placed(key, array):
        space = pltpu.HBM if key in outside else pltpu.VMEM
        return pltpu.with_memory_space_constraint(array, space) if key in (*outside, *held) else array

    results = pl.pallas_call(
        run,
        name=name,
        in_specs=[pl.BlockSpec(memory_space=pltpu.SMEM)] * len(scalars) + [spec(k) for k in arrays],
        out_specs=[spec(k) for k in outs],
        out_shape=[
            pltpu.VMEM(*o) if k in held else jax.ShapeDtypeStruct(*o) for k, o in outs.items()
        ],
        scratch_shapes=list(scratch.values()),
        compiler_params=pltpu.CompilerParams(vmem_limit_bytes=24 << 20),
        cost_estimate=pl.CostEstimate(flops=flops, bytes_accessed=flops // 8, transcendentals=0),
    )(*scalars.values(), *(placed(k, a) for k, a in arrays.items()))
    return dict(zip(outs, results, strict=True))


def split_halves(ref, values):
    n = values.shape[0]
    ref[pl.ds(0, n, stride=2), :] = values[:, :HALF]
    ref[pl.ds(1, n, stride=2), :] = values[:, HALF:]


def products(index, offset, source, blocks, target, base=0, first=0, count=None):
    def step(t, carry):
        at = 2 * index(offset + t)
        piece = jnp.concatenate([source[pl.ds(at, 1), :], source[pl.ds(at + 1, 1), :]], axis=1)
        target[pl.ds(t, 1), :] = jnp.dot(
            piece.astype(bf16), blocks[base + t], preferred_element_type=f32
        )
        return carry

    count = target.shape[0] if count is None else count
    lax.fori_loop(first, first + count, step, 0, unroll=min(count, UNROLL))


def in_rows(total, first):
    row = lax.broadcasted_iota(jnp.int32, (16, HALF), 0)
    whole = jnp.full((16, HALF), total, f32)
    high = whole.astype(bf16).astype(f32)
    middle = (whole - high).astype(bf16).astype(f32)
    low = whole - high - middle
    zero = jnp.zeros_like(whole)
    return jnp.where(
        row == first,
        high,
        jnp.where(row == first + 1, middle, jnp.where(row == first + 2, low, zero)),
    )


def restarts(r, j):
    return r.ints[1, AT_RESTART + j] == 1


def taken_by(r, k):
    taken = jnp.int32(1)
    for j in range(k):
        taken = jnp.where(restarts(r, j), 1, taken + 1)
    return taken.astype(f32)


def pack(values, extra):
    parts = [values[:, :HALF], values[:, HALF:]] + ([] if extra is None else [extra])
    return jnp.concatenate([p.astype(bf16) for p in parts], axis=0)


def to_peers(r, live, extra):
    slot = lax.broadcasted_iota(jnp.int32, r.found.shape, 0)
    packed = pack(jnp.where(slot < live, r.found[...], 0.0), extra)
    for p in range(r.message.shape[0]):
        r.message[p] = packed


def average(r, k, new, old, now, row):
    if k > LAST_RESTART:
        now[...] = new
        return None
    is_restart = restarts(r, k)
    summed, anchor = (new, old) if k == 0 else (r.sum[...] + new, r.anchor[...])
    mean = summed / taken_by(r, k)
    gap = mean - anchor
    now[...] = jnp.where(is_restart, mean, new)
    if k < LAST_RESTART:
        r.anchor_out[...] = jnp.where(is_restart, mean, anchor)
        r.sum_out[...] = jnp.where(is_restart, 0.0, summed)
    return in_rows(jnp.sum(gap * gap), row)


def first_dual(r):
    slots = r.stored.shape[0]
    vectors = [
        pltpu.make_async_copy(getattr(r, v + "_stored"), getattr(r, v), r.vector_arrivals.at[i])
        for i, v in enumerate(VECTORS)
    ]
    copies = [
        pltpu.make_async_copy(
            r.stored.at[pl.ds(c * CHUNK, CHUNK)],
            r.blocks.at[pl.ds(c * CHUNK, CHUNK)],
            r.arrivals.at[c],
        )
        for c in range(slots // CHUNK)
    ]
    places = (r.rows, r.cols_line, r.rows_line, r.restart)
    indices = [
        pltpu.make_async_copy(stored, place, r.index_arrivals.at[i])
        for i, (stored, place) in enumerate(
            zip(
                (r.rows_stored, r.cols_line_stored, r.rows_line_stored, r.restart_stored),
                places,
                strict=True,
            )
        )
    ]
    for copy in (*indices, vectors[0], *copies, *vectors[1:]):
        copy.start()
    for copy in indices:
        copy.wait()
    here = jnp.broadcast_to(r.rows_line[...], r.picked.shape)
    row = lax.broadcasted_iota(jnp.int32, r.picked.shape, 0)
    slot = lax.broadcasted_iota(jnp.int32, r.picked.shape, 1)
    r.picked[...] = jnp.where((here == row) & (slot < r.live[0]), 1.0, 0.0).astype(bf16)
    vectors[0].wait()
    for c, copy in enumerate(copies):
        copy.wait()
        products(lambda i: r.rows[i], 0, r.y, r.blocks, r.found, 0, c * CHUNK, CHUNK)
        for t in range(c * CHUNK, (c + 1) * CHUNK):
            r.blocks[slots + t] = r.blocks[t].T
    row = lax.broadcasted_iota(jnp.int32, (16, HALF), 0)
    lane = lax.broadcasted_iota(jnp.int32, (1, HALF), 1)
    others = jnp.where(lane == AT_LIVE, r.live[0], 0)
    for j in range(ITERS):
        others = jnp.where(lane == AT_RESTART + j, r.restart[j], others)
    r.ints[0:1, :] = jnp.concatenate([r.cols_line[...], r.rows_line[...]], axis=1)
    r.ints[1:2, :] = others
    told = jnp.broadcast_to(r.ints[0:1, :].astype(f32), (16, HALF))
    to_peers(r, r.live[0], jnp.where(row == 0, told, 0.0))
    for copy in vectors[1:]:
        copy.wait()


def sum_columns(k, r):
    peers = r.arrived.shape[0]
    slots = r.lined.shape[0] // peers
    chosen = r.told if k == 0 else r.chosen
    has_tail = r.arrived.shape[1] > 2 * slots
    tail = jnp.zeros((16, HALF), f32)
    for p in range(peers):
        r.lined[p * slots : (p + 1) * slots, :HALF] = r.arrived[p, :slots, :]
        r.lined[p * slots : (p + 1) * slots, HALF:] = r.arrived[p, slots : 2 * slots, :]
        if has_tail:
            tail = tail + r.arrived[p, 2 * slots :, :].astype(f32)
    if k == 0:
        shape = (chosen.shape[0], HALF)
        block = lax.broadcasted_iota(jnp.int32, shape, 0).astype(f32)
        early = lax.broadcasted_iota(jnp.int32, (1, HALF), 1) < slots
        for p in range(0, peers, 2):
            pair = [r.arrived[q, 2 * slots :, :].astype(f32) for q in (p, p + 1)]
            told = jnp.where(early, pair[0][0:1, :], pltpu.roll(pair[1], slots, 1)[0:1, :])
            told = jnp.broadcast_to(told, shape)
            chosen[:, p * slots : (p + 2) * slots] = jnp.where(told == block, 1.0, 0.0).astype(bf16)
    n = chosen.shape[0]
    split_halves(r.half, jnp.dot(chosen[...], r.lined[...], preferred_element_type=f32))
    if has_tail:
        total = tail[1:2, :] + tail[2:3, :] + tail[3:4, :]
        r.half[2 * n : 2 * n + 8, :] = jnp.broadcast_to(total, (8, HALF))


def primal_step(k, total_cols, total_rows, r):
    n = r.cost.shape[0]
    omega = jnp.ones((1, HALF), f32) if k == 0 else r.omega[0:1, :]
    if 1 <= k <= LAST_RESTART + 1:
        drift_x = r.drift[0:1, :] / total_cols + epsilon
        drift_y = (r.here[n : n + 1, :] + r.there[n : n + 1, :]) / total_rows + epsilon
        later = jnp.sqrt(omega) * jnp.sqrt(jnp.sqrt(drift_x / drift_y))
        omega = jnp.where(restarts(r, k - 1), later, omega)
    r.omega_out[...] = jnp.broadcast_to(omega, r.omega_out.shape)
    step_primal = step_scale / omega
    dual_image = r.here[0:n, :] + r.there[0:n, :]
    x = r.x[...]
    x_next = jnp.minimum(
        jnp.maximum(x - step_primal * (r.cost[...] - dual_image), 0.0), r.bound[...]
    )
    r.extrap[...] = 2.0 * x_next - x
    extra = average(r, k, x_next, x, r.x_out, 0)
    products(lambda i: r.ints[0, i], AT_COLS, r.extrap, r.blocks, r.found, r.found.shape[0])
    values = r.found[...]
    high = values.astype(bf16)
    low = (values - high.astype(f32)).astype(bf16)
    picked = r.picked[...]
    image = jnp.dot(picked, low, preferred_element_type=f32) + jnp.dot(
        picked, high, preferred_element_type=f32
    )
    r.message[...] = pack(image, extra)


def dual_step(k, r):
    n = r.demand.shape[0] // 2
    step_dual = step_scale * r.omega[0:1, :]
    both = (r.own[...].astype(f32) + r.opposite[...].astype(f32)) + (
        r.before[...].astype(f32) + r.after[...].astype(f32)
    )
    r.image[pl.ds(0, n, stride=2), :] = both[0:n, :]
    r.image[pl.ds(1, n, stride=2), :] = both[n : 2 * n, :]
    y = r.y[...]
    y_next = jnp.maximum(y + step_dual * (r.demand[...] - r.image[...]), 0.0)
    if k == ITERS - 1:
        r.y_out[...] = y_next
        return
    if k <= LAST_RESTART:
        tail = both[2 * n :, :]
        r.drift_out[...] = jnp.broadcast_to(tail[0:1, :] + tail[1:2, :] + tail[2:3, :], (8, HALF))
    extra = average(r, k, y_next, y, r.y_out, 1)
    products(lambda i: r.ints[0, i], AT_ROWS, r.y_out, r.blocks, r.found)
    to_peers(r, r.ints[1, AT_LIVE], extra)


def shards(
    block_values,
    block_rows,
    block_cols,
    live_count,
    objective,
    upper_bound,
    demand,
    primal_start,
    dual_start,
    restart_at,
):
    blocks = block_values[0, 0]
    rows = block_rows[0, 0]
    cols = block_cols[0, 0]
    slots, size = blocks.shape[0], blocks.shape[1]
    peers = lax.axis_size(XY)
    depth = lax.axis_size("col")
    total_cols = objective.shape[0] * depth
    total_rows = demand.shape[0] * lax.axis_size(ROW)
    stored = {
        name: vector.reshape(-1, HALF)
        for name, vector in zip(
            VECTORS, (dual_start, demand, objective, upper_bound, primal_start), strict=True
        )
    }
    n_rows, n_cols = demand.shape[0] // size, objective.shape[0] // size
    big, small, one = ((2 * n_cols, HALF), f32), ((2 * n_rows, HALF), f32), ((8, HALF), f32)

    def to_all(k):
        return ((peers, 2 * slots + 16 * (k <= LAST_RESTART), HALF), bf16)

    def to_column(k):
        return ((2 * n_rows + 16 * (k <= LAST_RESTART), HALF), bf16)

    chosen = ((n_cols, peers * slots), bf16)
    found = pltpu.VMEM((slots, size), f32)
    work = 2 * slots * size * size * 8
    lines = {
        "rows_stored": rows,
        "cols_line_stored": cols.reshape(1, -1),
        "rows_line_stored": rows.reshape(1, -1),
        "restart_stored": restart_at,
    }
    made = call(
        first_dual,
        "first_dual",
        {"live": live_count[0]},
        {"stored": blocks} | lines | {v + "_stored": a for v, a in stored.items()},
        {
            "blocks": ((2 * slots, size, size), bf16),
            "message": to_all(0),
            "picked": ((n_rows, slots), bf16),
            "ints": ((2, HALF), jnp.int32),
        }
        | {v: (a.shape, f32) for v, a in stored.items()},
        {
            "found": found,
            "arrivals": pltpu.SemaphoreType.DMA((slots // CHUNK,)),
            "vector_arrivals": pltpu.SemaphoreType.DMA((len(VECTORS),)),
            "index_arrivals": pltpu.SemaphoreType.DMA((4,)),
            "restart": pltpu.SMEM((ITERS,), jnp.int32),
            "rows": pltpu.SMEM((slots,), jnp.int32),
            "cols_line": pltpu.VMEM((1, slots), jnp.int32),
            "rows_line": pltpu.VMEM((1, slots), jnp.int32),
        },
        ("stored", *lines, *(v + "_stored" for v in VECTORS)),
        ("blocks", "ints", *VECTORS),
        work,
    )
    blocks, message, picked = made["blocks"], made["message"], made["picked"]
    ints = {"ints": made["ints"]}
    y, want, cost, bound, x = (made[v] for v in VECTORS)
    state_x, state_y, omega, drift, told = {}, {}, {}, {}, {}
    for k in range(ITERS):
        arrived = lax.all_to_all(message, XY, 0, 0, tiled=True)
        made = call(
            functools.partial(sum_columns, k),
            f"sum_columns_{k}",
            {},
            {"arrived": arrived} | told,
            {"half": ((2 * n_cols + 8 * (k <= LAST_RESTART + 1), HALF), f32)}
            | ({"told": chosen} if k == 0 else {}),
            {"lined": pltpu.VMEM((peers * slots, size), bf16)},
        )
        here = made["half"]
        if k == 0:
            told = {"chosen": made["told"]}
        there = lax.ppermute(here, CORE, [(0, 1), (1, 0)])
        averaged = k < LAST_RESTART
        sums = ("sum_out", "anchor_out") if averaged else ()
        if k > LAST_RESTART:
            state_x, state_y = {}, {}
        made = call(
            functools.partial(primal_step, k, total_cols, total_rows),
            f"primal_step_{k}",
            ints,
            {"here": here, "there": there, "cost": cost, "bound": bound, "x": x}
            | state_x
            | omega
            | drift
            | {"picked": picked, "blocks": blocks},
            {"x_out": big, "omega_out": one, "message": to_column(k)} | dict.fromkeys(sums, big),
            {"extrap": pltpu.VMEM(*big), "found": found},
            held=("blocks",) + ("x_out",) * (k == ITERS - 1),
            flops=work,
        )
        x, part, omega = made["x_out"], made["message"], {"omega": made["omega_out"]}
        if averaged:
            state_x = {"sum": made["sum_out"], "anchor": made["anchor_out"]}
        after, before, opposite = (
            lax.ppermute(part, "col", [(i, (i + d) % depth) for i in range(depth)])
            for d in (1, 3, 2)
        )
        parts = {"own": part, "after": after, "before": before, "opposite": opposite}
        image = {"image": pltpu.VMEM(*small)}
        if k == ITERS - 1:
            made = call(
                functools.partial(dual_step, k),
                f"dual_step_{k}",
                {},
                parts | {"demand": want, "y": y} | omega,
                {"y_out": small},
                image,
            )
            y = made["y_out"]
        else:
            made = call(
                functools.partial(dual_step, k),
                f"dual_step_{k}",
                ints,
                parts | {"demand": want, "y": y} | omega | state_y | {"blocks": blocks},
                {"y_out": small, "message": to_all(k)}
                | ({"drift_out": one} if k <= LAST_RESTART else {})
                | dict.fromkeys(sums, small),
                image | {"found": found},
                held=("blocks",),
                flops=work,
            )
            y, message = made["y_out"], made["message"]
            drift = {"drift": made["drift_out"]} if k <= LAST_RESTART else {}
            if averaged:
                state_y = {"sum": made["sum_out"], "anchor": made["anchor_out"]}
    return (x.reshape(-1), y.reshape(-1))


def solution(mesh):
    torus = Mesh(
        mesh.devices.reshape(4, 4, 2, mesh.shape["col"]), ("row_0", "row_1", "row_2", "col")
    )
    return jax.shard_map(
        shards,
        mesh=torus,
        in_specs=(
            P(ROW, "col", None, None, None),
            P(ROW, "col", None),
            P(ROW, "col", None),
            P(ROW, "col"),
            P("col"),
            P("col"),
            P(ROW),
            P("col"),
            P(ROW),
            P(),
        ),
        out_specs=(P("col"), P(ROW)),
        check_vma=False,
    )
```

```python
import functools
import types

import jax
import jax.numpy as jnp
from jax import lax
from jax.experimental import pallas as pl
from jax.experimental.pallas import tpu as pltpu
from jax.sharding import Mesh
from jax.sharding import PartitionSpec as P

ITERS = 8
XY = ("row_0", "row_1")
CORE = "row_2"
ROW = ("row_0", "row_1", "row_2")
HALF = 128
CHUNK = 16
UNROLL = 64
LAST_RESTART = ITERS - 3
AT_COLS, AT_ROWS, AT_LIVE, AT_RESTART = 0, 64, 0, 8

step_scale = 0.3
epsilon = 1e-06

f32, bf16 = jnp.float32, jnp.bfloat16
VECTORS = ("y", "demand", "cost", "bound", "x")


def call(body, name, scalars, arrays, outs, scratch, outside=(), held=(), flops=0):
    names = [*scalars, *arrays, *outs, *scratch]

    def run(*refs):
        body(types.SimpleNamespace(**dict(zip(names, refs, strict=True))))

    def spec(key):
        return pl.BlockSpec(memory_space=pltpu.HBM if key in outside else pltpu.VMEM)

    def placed(key, array):
        space = pltpu.HBM if key in outside else pltpu.VMEM
        return pltpu.with_memory_space_constraint(array, space) if key in (*outside, *held) else array

    results = pl.pallas_call(
        run,
        name=name,
        in_specs=[pl.BlockSpec(memory_space=pltpu.SMEM)] * len(scalars) + [spec(k) for k in arrays],
        out_specs=[spec(k) for k in outs],
        out_shape=[
            pltpu.VMEM(*o) if k in held else jax.ShapeDtypeStruct(*o) for k, o in outs.items()
        ],
        scratch_shapes=list(scratch.values()),
        compiler_params=pltpu.CompilerParams(vmem_limit_bytes=24 << 20),
        cost_estimate=pl.CostEstimate(flops=flops, bytes_accessed=flops // 8, transcendentals=0),
    )(*scalars.values(), *(placed(k, a) for k, a in arrays.items()))
    return dict(zip(outs, results, strict=True))


def split_halves(ref, values):
    n = values.shape[0]
    ref[pl.ds(0, n, stride=2), :] = values[:, :HALF]
    ref[pl.ds(1, n, stride=2), :] = values[:, HALF:]


def products(index, offset, source, blocks, target, base=0, first=0, count=None):
    def step(t, carry):
        at = 2 * index(offset + t)
        piece = jnp.concatenate([source[pl.ds(at, 1), :], source[pl.ds(at + 1, 1), :]], axis=1)
        target[pl.ds(t, 1), :] = jnp.dot(
            piece.astype(bf16), blocks[base + t], preferred_element_type=f32
        )
        return carry

    count = target.shape[0] if count is None else count
    lax.fori_loop(first, first + count, step, 0, unroll=min(count, UNROLL))


def in_rows(total, first):
    row = lax.broadcasted_iota(jnp.int32, (16, HALF), 0)
    whole = jnp.full((16, HALF), total, f32)
    high = whole.astype(bf16).astype(f32)
    middle = (whole - high).astype(bf16).astype(f32)
    low = whole - high - middle
    zero = jnp.zeros_like(whole)
    return jnp.where(
        row == first,
        high,
        jnp.where(row == first + 1, middle, jnp.where(row == first + 2, low, zero)),
    )


def restarts(r, j):
    return r.ints[1, AT_RESTART + j] == 1


def taken_by(r, k):
    taken = jnp.int32(1)
    for j in range(k):
        taken = jnp.where(restarts(r, j), 1, taken + 1)
    return taken.astype(f32)


def pack(values, extra):
    parts = [values[:, :HALF], values[:, HALF:]] + ([] if extra is None else [extra])
    return jnp.concatenate([p.astype(bf16) for p in parts], axis=0)


def to_peers(r, live, extra):
    slot = lax.broadcasted_iota(jnp.int32, r.found.shape, 0)
    packed = pack(jnp.where(slot < live, r.found[...], 0.0), extra)
    for p in range(r.message.shape[0]):
        r.message[p] = packed


def average(r, k, new, old, now, row):
    if k > LAST_RESTART:
        now[...] = new
        return None
    is_restart = restarts(r, k)
    summed, anchor = (new, old) if k == 0 else (r.sum[...] + new, r.anchor[...])
    mean = summed / taken_by(r, k)
    gap = mean - anchor
    now[...] = jnp.where(is_restart, mean, new)
    if k < LAST_RESTART:
        r.anchor_out[...] = jnp.where(is_restart, mean, anchor)
        r.sum_out[...] = jnp.where(is_restart, 0.0, summed)
    return in_rows(jnp.sum(gap * gap), row)


def first_dual(r):
    slots = r.stored.shape[0]
    vectors = [
        pltpu.make_async_copy(getattr(r, v + "_stored"), getattr(r, v), r.vector_arrivals.at[i])
        for i, v in enumerate(VECTORS)
    ]
    copies = [
        pltpu.make_async_copy(
            r.stored.at[pl.ds(c * CHUNK, CHUNK)],
            r.blocks.at[pl.ds(c * CHUNK, CHUNK)],
            r.arrivals.at[c],
        )
        for c in range(slots // CHUNK)
    ]
    places = (r.rows, r.cols_line, r.rows_line, r.restart)
    indices = [
        pltpu.make_async_copy(stored, place, r.index_arrivals.at[i])
        for i, (stored, place) in enumerate(
            zip(
                (r.rows_stored, r.cols_line_stored, r.rows_line_stored, r.restart_stored),
                places,
                strict=True,
            )
        )
    ]
    for copy in (*indices, vectors[0], *copies, *vectors[1:]):
        copy.start()
    for copy in indices:
        copy.wait()
    here = jnp.broadcast_to(r.rows_line[...], r.picked.shape)
    row = lax.broadcasted_iota(jnp.int32, r.picked.shape, 0)
    slot = lax.broadcasted_iota(jnp.int32, r.picked.shape, 1)
    r.picked[...] = jnp.where((here == row) & (slot < r.live[0]), 1.0, 0.0).astype(bf16)
    vectors[0].wait()
    for c, copy in enumerate(copies):
        copy.wait()
        products(lambda i: r.rows[i], 0, r.y, r.blocks, r.found, 0, c * CHUNK, CHUNK)
        for t in range(c * CHUNK, (c + 1) * CHUNK):
            r.blocks[slots + t] = r.blocks[t].T
    row = lax.broadcasted_iota(jnp.int32, (16, HALF), 0)
    lane = lax.broadcasted_iota(jnp.int32, (1, HALF), 1)
    others = jnp.where(lane == AT_LIVE, r.live[0], 0)
    for j in range(ITERS):
        others = jnp.where(lane == AT_RESTART + j, r.restart[j], others)
    r.ints[0:1, :] = jnp.concatenate([r.cols_line[...], r.rows_line[...]], axis=1)
    r.ints[1:2, :] = others
    told = jnp.broadcast_to(r.ints[0:1, :].astype(f32), (16, HALF))
    to_peers(r, r.live[0], jnp.where(row == 0, told, 0.0))
    for copy in vectors[1:]:
        copy.wait()


def sum_columns(k, r):
    peers = r.arrived.shape[0]
    chosen = r.told if k == 0 else r.chosen
    slots = chosen.shape[1] // peers
    has_tail = r.arrived.shape[1] > 2 * slots
    tail = jnp.zeros((16, HALF), f32)
    for p in range(peers):
        if has_tail:
            tail = tail + r.arrived[p, 2 * slots :, :].astype(f32)
    if k == 0:
        shape = (chosen.shape[0], HALF)
        block = lax.broadcasted_iota(jnp.int32, shape, 0).astype(f32)
        early = lax.broadcasted_iota(jnp.int32, (1, HALF), 1) < slots
        for p in range(0, peers, 2):
            pair = [r.arrived[q, 2 * slots :, :].astype(f32) for q in (p, p + 1)]
            told = jnp.where(early, pair[0][0:1, :], pltpu.roll(pair[1], slots, 1)[0:1, :])
            told = jnp.broadcast_to(told, shape)
            chosen[:, p * slots : (p + 2) * slots] = jnp.where(told == block, 1.0, 0.0).astype(bf16)
    n = chosen.shape[0]
    lined = [
        jnp.concatenate([r.arrived[p, :slots, :], r.arrived[p, slots : 2 * slots, :]], axis=1)
        for p in range(peers)
    ]
    split_halves(
        r.half,
        jnp.dot(chosen[...], jnp.concatenate(lined, axis=0), preferred_element_type=f32),
    )
    if has_tail:
        total = tail[1:2, :] + tail[2:3, :] + tail[3:4, :]
        r.half[2 * n : 2 * n + 8, :] = jnp.broadcast_to(total, (8, HALF))


def primal_step(k, total_cols, total_rows, r):
    n = r.cost.shape[0]
    omega = jnp.ones((1, HALF), f32) if k == 0 else r.omega[0:1, :]
    if 1 <= k <= LAST_RESTART + 1:
        drift_x = r.drift[0:1, :] / total_cols + epsilon
        drift_y = (r.here[n : n + 1, :] + r.there[n : n + 1, :]) / total_rows + epsilon
        later = jnp.sqrt(omega) * jnp.sqrt(jnp.sqrt(drift_x / drift_y))
        omega = jnp.where(restarts(r, k - 1), later, omega)
    r.omega_out[...] = jnp.broadcast_to(omega, r.omega_out.shape)
    step_primal = step_scale / omega
    dual_image = r.here[0:n, :] + r.there[0:n, :]
    x = r.x[...]
    x_next = jnp.minimum(
        jnp.maximum(x - step_primal * (r.cost[...] - dual_image), 0.0), r.bound[...]
    )
    r.extrap[...] = 2.0 * x_next - x
    extra = average(r, k, x_next, x, r.x_out, 0)
    products(lambda i: r.ints[0, i], AT_COLS, r.extrap, r.blocks, r.found, r.found.shape[0])
    values = r.found[...]
    high = values.astype(bf16)
    low = (values - high.astype(f32)).astype(bf16)
    picked = r.picked[...]
    image = jnp.dot(picked, low, preferred_element_type=f32) + jnp.dot(
        picked, high, preferred_element_type=f32
    )
    r.message[...] = pack(image, extra)


def dual_step(k, r):
    n = r.demand.shape[0] // 2
    step_dual = step_scale * r.omega[0:1, :]
    both = (r.own[...].astype(f32) + r.opposite[...].astype(f32)) + (
        r.before[...].astype(f32) + r.after[...].astype(f32)
    )
    r.image[pl.ds(0, n, stride=2), :] = both[0:n, :]
    r.image[pl.ds(1, n, stride=2), :] = both[n : 2 * n, :]
    y = r.y[...]
    y_next = jnp.maximum(y + step_dual * (r.demand[...] - r.image[...]), 0.0)
    if k == ITERS - 1:
        r.y_out[...] = y_next
        return
    if k <= LAST_RESTART:
        tail = both[2 * n :, :]
        r.drift_out[...] = jnp.broadcast_to(tail[0:1, :] + tail[1:2, :] + tail[2:3, :], (8, HALF))
    extra = average(r, k, y_next, y, r.y_out, 1)
    products(lambda i: r.ints[0, i], AT_ROWS, r.y_out, r.blocks, r.found)
    to_peers(r, r.ints[1, AT_LIVE], extra)


def shards(
    block_values,
    block_rows,
    block_cols,
    live_count,
    objective,
    upper_bound,
    demand,
    primal_start,
    dual_start,
    restart_at,
):
    blocks = block_values[0, 0]
    rows = block_rows[0, 0]
    cols = block_cols[0, 0]
    slots, size = blocks.shape[0], blocks.shape[1]
    peers = lax.axis_size(XY)
    depth = lax.axis_size("col")
    total_cols = objective.shape[0] * depth
    total_rows = demand.shape[0] * lax.axis_size(ROW)
    stored = {
        name: vector.reshape(-1, HALF)
        for name, vector in zip(
            VECTORS, (dual_start, demand, objective, upper_bound, primal_start), strict=True
        )
    }
    n_rows, n_cols = demand.shape[0] // size, objective.shape[0] // size
    big, small, one = ((2 * n_cols, HALF), f32), ((2 * n_rows, HALF), f32), ((8, HALF), f32)

    def to_all(k):
        return ((peers, 2 * slots + 16 * (k <= LAST_RESTART), HALF), bf16)

    def to_column(k):
        return ((2 * n_rows + 16 * (k <= LAST_RESTART), HALF), bf16)

    chosen = ((n_cols, peers * slots), bf16)
    found = pltpu.VMEM((slots, size), f32)
    work = 2 * slots * size * size * 8
    lines = {
        "rows_stored": rows,
        "cols_line_stored": cols.reshape(1, -1),
        "rows_line_stored": rows.reshape(1, -1),
        "restart_stored": restart_at,
    }
    made = call(
        first_dual,
        "first_dual",
        {"live": live_count[0]},
        {"stored": blocks} | lines | {v + "_stored": a for v, a in stored.items()},
        {
            "blocks": ((2 * slots, size, size), bf16),
            "message": to_all(0),
            "picked": ((n_rows, slots), bf16),
            "ints": ((2, HALF), jnp.int32),
        }
        | {v: (a.shape, f32) for v, a in stored.items()},
        {
            "found": found,
            "arrivals": pltpu.SemaphoreType.DMA((slots // CHUNK,)),
            "vector_arrivals": pltpu.SemaphoreType.DMA((len(VECTORS),)),
            "index_arrivals": pltpu.SemaphoreType.DMA((4,)),
            "restart": pltpu.SMEM((ITERS,), jnp.int32),
            "rows": pltpu.SMEM((slots,), jnp.int32),
            "cols_line": pltpu.VMEM((1, slots), jnp.int32),
            "rows_line": pltpu.VMEM((1, slots), jnp.int32),
        },
        ("stored", *lines, *(v + "_stored" for v in VECTORS)),
        ("blocks", "ints", *VECTORS),
        work,
    )
    blocks, message, picked = made["blocks"], made["message"], made["picked"]
    ints = {"ints": made["ints"]}
    y, want, cost, bound, x = (made[v] for v in VECTORS)
    state_x, state_y, omega, drift, told = {}, {}, {}, {}, {}
    for k in range(ITERS):
        arrived = lax.all_to_all(message, XY, 0, 0, tiled=True)
        made = call(
            functools.partial(sum_columns, k),
            f"sum_columns_{k}",
            {},
            {"arrived": arrived} | told,
            {"half": ((2 * n_cols + 8 * (k <= LAST_RESTART + 1), HALF), f32)}
            | ({"told": chosen} if k == 0 else {}),
            {},
        )
        here = made["half"]
        if k == 0:
            told = {"chosen": made["told"]}
        there = lax.ppermute(here, CORE, [(0, 1), (1, 0)])
        averaged = k < LAST_RESTART
        sums = ("sum_out", "anchor_out") if averaged else ()
        if k > LAST_RESTART:
            state_x, state_y = {}, {}
        made = call(
            functools.partial(primal_step, k, total_cols, total_rows),
            f"primal_step_{k}",
            ints,
            {"here": here, "there": there, "cost": cost, "bound": bound, "x": x}
            | state_x
            | omega
            | drift
            | {"picked": picked, "blocks": blocks},
            {"x_out": big, "omega_out": one, "message": to_column(k)} | dict.fromkeys(sums, big),
            {"extrap": pltpu.VMEM(*big), "found": found},
            held=("blocks",) + ("x_out",) * (k == ITERS - 1),
            flops=work,
        )
        x, part, omega = made["x_out"], made["message"], {"omega": made["omega_out"]}
        if averaged:
            state_x = {"sum": made["sum_out"], "anchor": made["anchor_out"]}
        after, before, opposite = (
            lax.ppermute(part, "col", [(i, (i + d) % depth) for i in range(depth)])
            for d in (1, 3, 2)
        )
        parts = {"own": part, "before": before, "after": after, "opposite": opposite}
        image = {"image": pltpu.VMEM(*small)}
        if k == ITERS - 1:
            made = call(
                functools.partial(dual_step, k),
                f"dual_step_{k}",
                {},
                parts | {"demand": want, "y": y} | omega,
                {"y_out": small},
                image,
            )
            y = made["y_out"]
        else:
            made = call(
                functools.partial(dual_step, k),
                f"dual_step_{k}",
                ints,
                parts | {"demand": want, "y": y} | omega | state_y | {"blocks": blocks},
                {"y_out": small, "message": to_all(k)}
                | ({"drift_out": one} if k <= LAST_RESTART else {})
                | dict.fromkeys(sums, small),
                image | {"found": found},
                held=("blocks",),
                flops=work,
            )
            y, message = made["y_out"], made["message"]
            drift = {"drift": made["drift_out"]} if k <= LAST_RESTART else {}
            if averaged:
                state_y = {"sum": made["sum_out"], "anchor": made["anchor_out"]}
    return (x.reshape(-1), y.reshape(-1))


def solution(mesh):
    torus = Mesh(
        mesh.devices.reshape(4, 4, 2, mesh.shape["col"]), ("row_0", "row_1", "row_2", "col")
    )
    return jax.shard_map(
        shards,
        mesh=torus,
        in_specs=(
            P(ROW, "col", None, None, None),
            P(ROW, "col", None),
            P(ROW, "col", None),
            P(ROW, "col"),
            P("col"),
            P("col"),
            P(ROW),
            P("col"),
            P(ROW),
            P(),
        ),
        out_specs=(P("col"), P(ROW)),
        check_vma=False,
    )
```

```python
import functools
import types

import jax
import jax.numpy as jnp
from jax import lax
from jax.experimental import pallas as pl
from jax.experimental.pallas import tpu as pltpu
from jax.sharding import Mesh
from jax.sharding import PartitionSpec as P

ITERS = 8
XY = ("row_0", "row_1")
CORE = "row_2"
ROW = ("row_0", "row_1", "row_2")
HALF = 128
CHUNK = 32
UNROLL = 64
LAST_RESTART = ITERS - 3
AT_COLS, AT_ROWS, AT_LIVE, AT_RESTART = 0, 64, 0, 8

step_scale = 0.3
epsilon = 1e-06

f32, bf16 = jnp.float32, jnp.bfloat16
VECTORS = ("y", "demand", "cost", "bound", "x")


def call(body, name, scalars, arrays, outs, scratch, outside=(), held=(), flops=0):
    names = [*scalars, *arrays, *outs, *scratch]

    def run(*refs):
        body(types.SimpleNamespace(**dict(zip(names, refs, strict=True))))

    def spec(key):
        return pl.BlockSpec(memory_space=pltpu.HBM if key in outside else pltpu.VMEM)

    def placed(key, array):
        space = pltpu.HBM if key in outside else pltpu.VMEM
        return pltpu.with_memory_space_constraint(array, space) if key in (*outside, *held) else array

    results = pl.pallas_call(
        run,
        name=name,
        in_specs=[pl.BlockSpec(memory_space=pltpu.SMEM)] * len(scalars) + [spec(k) for k in arrays],
        out_specs=[spec(k) for k in outs],
        out_shape=[
            pltpu.VMEM(*o) if k in held else jax.ShapeDtypeStruct(*o) for k, o in outs.items()
        ],
        scratch_shapes=list(scratch.values()),
        compiler_params=pltpu.CompilerParams(vmem_limit_bytes=24 << 20),
        cost_estimate=pl.CostEstimate(flops=flops, bytes_accessed=flops // 8, transcendentals=0),
    )(*scalars.values(), *(placed(k, a) for k, a in arrays.items()))
    return dict(zip(outs, results, strict=True))


def split_halves(ref, values):
    n = values.shape[0]
    ref[pl.ds(0, n, stride=2), :] = values[:, :HALF]
    ref[pl.ds(1, n, stride=2), :] = values[:, HALF:]


def products(index, offset, source, blocks, target, base=0, first=0, count=None):
    def step(t, carry):
        at = 2 * index(offset + t)
        piece = jnp.concatenate([source[pl.ds(at, 1), :], source[pl.ds(at + 1, 1), :]], axis=1)
        target[pl.ds(t, 1), :] = jnp.dot(
            piece.astype(bf16), blocks[base + t], preferred_element_type=f32
        )
        return carry

    count = target.shape[0] if count is None else count
    lax.fori_loop(first, first + count, step, 0, unroll=min(count, UNROLL))


def in_rows(total, first):
    row = lax.broadcasted_iota(jnp.int32, (16, HALF), 0)
    whole = jnp.full((16, HALF), total, f32)
    high = whole.astype(bf16).astype(f32)
    middle = (whole - high).astype(bf16).astype(f32)
    low = whole - high - middle
    zero = jnp.zeros_like(whole)
    return jnp.where(
        row == first,
        high,
        jnp.where(row == first + 1, middle, jnp.where(row == first + 2, low, zero)),
    )


def restarts(r, j):
    return r.ints[1, AT_RESTART + j] == 1


def taken_by(r, k):
    taken = jnp.int32(1)
    for j in range(k):
        taken = jnp.where(restarts(r, j), 1, taken + 1)
    return taken.astype(f32)


def pack(values, extra):
    parts = [values[:, :HALF], values[:, HALF:]] + ([] if extra is None else [extra])
    return jnp.concatenate([p.astype(bf16) for p in parts], axis=0)


def to_peers(r, live, extra):
    slot = lax.broadcasted_iota(jnp.int32, r.found.shape, 0)
    packed = pack(jnp.where(slot < live, r.found[...], 0.0), extra)
    for p in range(r.message.shape[0]):
        r.message[p] = packed


def average(r, k, new, old, now, row):
    if k > LAST_RESTART:
        now[...] = new
        return None
    is_restart = restarts(r, k)
    summed, anchor = (new, old) if k == 0 else (r.sum[...] + new, r.anchor[...])
    mean = summed / taken_by(r, k)
    gap = mean - anchor
    now[...] = jnp.where(is_restart, mean, new)
    if k < LAST_RESTART:
        r.anchor_out[...] = jnp.where(is_restart, mean, anchor)
        r.sum_out[...] = jnp.where(is_restart, 0.0, summed)
    return in_rows(jnp.sum(gap * gap), row)


def first_dual(r):
    slots = r.stored.shape[0]
    vectors = [
        pltpu.make_async_copy(getattr(r, v + "_stored"), getattr(r, v), r.vector_arrivals.at[i])
        for i, v in enumerate(VECTORS)
    ]
    copies = [
        pltpu.make_async_copy(
            r.stored.at[pl.ds(c * CHUNK, CHUNK)],
            r.blocks.at[pl.ds(c * CHUNK, CHUNK)],
            r.arrivals.at[c],
        )
        for c in range(slots // CHUNK)
    ]
    places = (r.rows, r.cols_line, r.rows_line, r.restart)
    indices = [
        pltpu.make_async_copy(stored, place, r.index_arrivals.at[i])
        for i, (stored, place) in enumerate(
            zip(
                (r.rows_stored, r.cols_line_stored, r.rows_line_stored, r.restart_stored),
                places,
                strict=True,
            )
        )
    ]
    for copy in (*indices, vectors[0], *copies, *vectors[1:]):
        copy.start()
    for copy in indices:
        copy.wait()
    here = jnp.broadcast_to(r.rows_line[...], r.picked.shape)
    row = lax.broadcasted_iota(jnp.int32, r.picked.shape, 0)
    slot = lax.broadcasted_iota(jnp.int32, r.picked.shape, 1)
    r.picked[...] = jnp.where((here == row) & (slot < r.live[0]), 1.0, 0.0).astype(bf16)
    vectors[0].wait()
    for c, copy in enumerate(copies):
        copy.wait()
        products(lambda i: r.rows[i], 0, r.y, r.blocks, r.found, 0, c * CHUNK, CHUNK)
        for t in range(c * CHUNK, (c + 1) * CHUNK):
            r.blocks[slots + t] = r.blocks[t].T
    row = lax.broadcasted_iota(jnp.int32, (16, HALF), 0)
    lane = lax.broadcasted_iota(jnp.int32, (1, HALF), 1)
    others = jnp.where(lane == AT_LIVE, r.live[0], 0)
    for j in range(ITERS):
        others = jnp.where(lane == AT_RESTART + j, r.restart[j], others)
    r.ints[0:1, :] = jnp.concatenate([r.cols_line[...], r.rows_line[...]], axis=1)
    r.ints[1:2, :] = others
    told = jnp.broadcast_to(r.ints[0:1, :].astype(f32), (16, HALF))
    to_peers(r, r.live[0], jnp.where(row == 0, told, 0.0))
    for copy in vectors[1:]:
        copy.wait()


def sum_columns(k, r):
    peers = r.arrived.shape[0]
    chosen = r.told if k == 0 else r.chosen
    slots = chosen.shape[1] // peers
    has_tail = r.arrived.shape[1] > 2 * slots
    tail = jnp.zeros((16, HALF), f32)
    for p in range(peers):
        if has_tail:
            tail = tail + r.arrived[p, 2 * slots :, :].astype(f32)
    if k == 0:
        shape = (chosen.shape[0], HALF)
        block = lax.broadcasted_iota(jnp.int32, shape, 0).astype(f32)
        early = lax.broadcasted_iota(jnp.int32, (1, HALF), 1) < slots
        for p in range(0, peers, 2):
            pair = [r.arrived[q, 2 * slots :, :].astype(f32) for q in (p, p + 1)]
            told = jnp.where(early, pair[0][0:1, :], pltpu.roll(pair[1], slots, 1)[0:1, :])
            told = jnp.broadcast_to(told, shape)
            chosen[:, p * slots : (p + 2) * slots] = jnp.where(told == block, 1.0, 0.0).astype(bf16)
    n = chosen.shape[0]
    lined = [
        jnp.concatenate([r.arrived[p, :slots, :], r.arrived[p, slots : 2 * slots, :]], axis=1)
        for p in range(peers)
    ]
    split_halves(
        r.half,
        jnp.dot(chosen[...], jnp.concatenate(lined, axis=0), preferred_element_type=f32),
    )
    if has_tail:
        total = tail[1:2, :] + tail[2:3, :] + tail[3:4, :]
        r.half[2 * n : 2 * n + 8, :] = jnp.broadcast_to(total, (8, HALF))


def primal_step(k, total_cols, total_rows, r):
    n = r.cost.shape[0]
    omega = jnp.ones((1, HALF), f32) if k == 0 else r.omega[0:1, :]
    if 1 <= k <= LAST_RESTART + 1:
        drift_x = r.drift[0:1, :] / total_cols + epsilon
        drift_y = (r.here[n : n + 1, :] + r.there[n : n + 1, :]) / total_rows + epsilon
        later = jnp.sqrt(omega) * jnp.sqrt(jnp.sqrt(drift_x / drift_y))
        omega = jnp.where(restarts(r, k - 1), later, omega)
    r.omega_out[...] = jnp.broadcast_to(omega, r.omega_out.shape)
    step_primal = step_scale / omega
    dual_image = r.here[0:n, :] + r.there[0:n, :]
    x = r.x[...]
    x_next = jnp.minimum(
        jnp.maximum(x - step_primal * (r.cost[...] - dual_image), 0.0), r.bound[...]
    )
    r.extrap[...] = 2.0 * x_next - x
    extra = average(r, k, x_next, x, r.x_out, 0)
    products(lambda i: r.ints[0, i], AT_COLS, r.extrap, r.blocks, r.found, r.found.shape[0])
    values = r.found[...]
    high = values.astype(bf16)
    low = (values - high.astype(f32)).astype(bf16)
    picked = r.picked[...]
    image = jnp.dot(picked, low, preferred_element_type=f32) + jnp.dot(
        picked, high, preferred_element_type=f32
    )
    r.message[...] = pack(image, extra)


def dual_step(k, r):
    n = r.demand.shape[0] // 2
    step_dual = step_scale * r.omega[0:1, :]
    both = (r.own[...].astype(f32) + r.opposite[...].astype(f32)) + (
        r.before[...].astype(f32) + r.after[...].astype(f32)
    )
    r.image[pl.ds(0, n, stride=2), :] = both[0:n, :]
    r.image[pl.ds(1, n, stride=2), :] = both[n : 2 * n, :]
    y = r.y[...]
    y_next = jnp.maximum(y + step_dual * (r.demand[...] - r.image[...]), 0.0)
    if k == ITERS - 1:
        r.y_out[...] = y_next
        return
    if k <= LAST_RESTART:
        tail = both[2 * n :, :]
        r.drift_out[...] = jnp.broadcast_to(tail[0:1, :] + tail[1:2, :] + tail[2:3, :], (8, HALF))
    extra = average(r, k, y_next, y, r.y_out, 1)
    products(lambda i: r.ints[0, i], AT_ROWS, r.y_out, r.blocks, r.found)
    to_peers(r, r.ints[1, AT_LIVE], extra)


def shards(
    block_values,
    block_rows,
    block_cols,
    live_count,
    objective,
    upper_bound,
    demand,
    primal_start,
    dual_start,
    restart_at,
):
    blocks = block_values[0, 0]
    rows = block_rows[0, 0]
    cols = block_cols[0, 0]
    slots, size = blocks.shape[0], blocks.shape[1]
    peers = lax.axis_size(XY)
    depth = lax.axis_size("col")
    total_cols = objective.shape[0] * depth
    total_rows = demand.shape[0] * lax.axis_size(ROW)
    stored = {
        name: vector.reshape(-1, HALF)
        for name, vector in zip(
            VECTORS, (dual_start, demand, objective, upper_bound, primal_start), strict=True
        )
    }
    n_rows, n_cols = demand.shape[0] // size, objective.shape[0] // size
    big, small, one = ((2 * n_cols, HALF), f32), ((2 * n_rows, HALF), f32), ((8, HALF), f32)

    def to_all(k):
        return ((peers, 2 * slots + 16 * (k <= LAST_RESTART), HALF), bf16)

    def to_column(k):
        return ((2 * n_rows + 16 * (k <= LAST_RESTART), HALF), bf16)

    chosen = ((n_cols, peers * slots), bf16)
    found = pltpu.VMEM((slots, size), f32)
    work = 2 * slots * size * size * 8
    lines = {
        "rows_stored": rows,
        "cols_line_stored": cols.reshape(1, -1),
        "rows_line_stored": rows.reshape(1, -1),
        "restart_stored": restart_at,
    }
    made = call(
        first_dual,
        "first_dual",
        {"live": live_count[0]},
        {"stored": blocks} | lines | {v + "_stored": a for v, a in stored.items()},
        {
            "blocks": ((2 * slots, size, size), bf16),
            "message": to_all(0),
            "picked": ((n_rows, slots), bf16),
            "ints": ((2, HALF), jnp.int32),
        }
        | {v: (a.shape, f32) for v, a in stored.items()},
        {
            "found": found,
            "arrivals": pltpu.SemaphoreType.DMA((slots // CHUNK,)),
            "vector_arrivals": pltpu.SemaphoreType.DMA((len(VECTORS),)),
            "index_arrivals": pltpu.SemaphoreType.DMA((4,)),
            "restart": pltpu.SMEM((ITERS,), jnp.int32),
            "rows": pltpu.SMEM((slots,), jnp.int32),
            "cols_line": pltpu.VMEM((1, slots), jnp.int32),
            "rows_line": pltpu.VMEM((1, slots), jnp.int32),
        },
        ("stored", *lines, *(v + "_stored" for v in VECTORS)),
        ("blocks", "ints", *VECTORS),
        work,
    )
    blocks, message, picked = made["blocks"], made["message"], made["picked"]
    ints = {"ints": made["ints"]}
    y, want, cost, bound, x = (made[v] for v in VECTORS)
    state_x, state_y, omega, drift, told = {}, {}, {}, {}, {}
    for k in range(ITERS):
        arrived = lax.all_to_all(message, XY, 0, 0, tiled=True)
        made = call(
            functools.partial(sum_columns, k),
            f"sum_columns_{k}",
            {},
            {"arrived": arrived} | told,
            {"half": ((2 * n_cols + 8 * (k <= LAST_RESTART + 1), HALF), f32)}
            | ({"told": chosen} if k == 0 else {}),
            {},
        )
        here = made["half"]
        if k == 0:
            told = {"chosen": made["told"]}
        there = lax.ppermute(here, CORE, [(0, 1), (1, 0)])
        averaged = k < LAST_RESTART
        sums = ("sum_out", "anchor_out") if averaged else ()
        if k > LAST_RESTART:
            state_x, state_y = {}, {}
        made = call(
            functools.partial(primal_step, k, total_cols, total_rows),
            f"primal_step_{k}",
            ints,
            {"here": here, "there": there, "cost": cost, "bound": bound, "x": x}
            | state_x
            | omega
            | drift
            | {"picked": picked, "blocks": blocks},
            {"x_out": big, "omega_out": one, "message": to_column(k)} | dict.fromkeys(sums, big),
            {"extrap": pltpu.VMEM(*big), "found": found},
            held=("blocks",) + ("x_out",) * (k == ITERS - 1),
            flops=work,
        )
        x, part, omega = made["x_out"], made["message"], {"omega": made["omega_out"]}
        if averaged:
            state_x = {"sum": made["sum_out"], "anchor": made["anchor_out"]}
        after, before, opposite = (
            lax.ppermute(part, "col", [(i, (i + d) % depth) for i in range(depth)])
            for d in (1, 3, 2)
        )
        parts = {"own": part, "before": before, "after": after, "opposite": opposite}
        image = {"image": pltpu.VMEM(*small)}
        if k == ITERS - 1:
            made = call(
                functools.partial(dual_step, k),
                f"dual_step_{k}",
                {},
                parts | {"demand": want, "y": y} | omega,
                {"y_out": small},
                image,
            )
            y = made["y_out"]
        else:
            made = call(
                functools.partial(dual_step, k),
                f"dual_step_{k}",
                ints,
                parts | {"demand": want, "y": y} | omega | state_y | {"blocks": blocks},
                {"y_out": small, "message": to_all(k)}
                | ({"drift_out": one} if k <= LAST_RESTART else {})
                | dict.fromkeys(sums, small),
                image | {"found": found},
                held=("blocks",),
                flops=work,
            )
            y, message = made["y_out"], made["message"]
            drift = {"drift": made["drift_out"]} if k <= LAST_RESTART else {}
            if averaged:
                state_y = {"sum": made["sum_out"], "anchor": made["anchor_out"]}
    return (x.reshape(-1), y.reshape(-1))


def solution(mesh):
    torus = Mesh(
        mesh.devices.reshape(4, 4, 2, mesh.shape["col"]), ("row_0", "row_1", "row_2", "col")
    )
    return jax.shard_map(
        shards,
        mesh=torus,
        in_specs=(
            P(ROW, "col", None, None, None),
            P(ROW, "col", None),
            P(ROW, "col", None),
            P(ROW, "col"),
            P("col"),
            P("col"),
            P(ROW),
            P("col"),
            P(ROW),
            P(),
        ),
        out_specs=(P("col"), P(ROW)),
        check_vma=False,
    )
```
